32 devices in a mesh: dp: 2 (over x), bytes: 16 (over z, y, core).
Axes of the slice: x: 2, y: 2, z: 4, core: 2. Of those that a mesh axis runs over, the one named last changes fastest.
Arguments:
- byte_queries: bfloat16 [2, 2048, 1024], P('dp', 'bytes'), may hold values from -48 to 48
- byte_keys: bfloat16 [2, 2048, 1024], P('dp', 'bytes'), may hold values from -6 to 6
- byte_values: bfloat16 [2, 2048, 1024], P('dp', 'bytes'), may hold values from -6 to 6
- patch_starts: int32 [2, 16, 12], P('dp', 'bytes'), may hold values from 0 to 128, as said below
- patch_proj: bfloat16 [1024, 4096], P('dp', 'bytes'), may hold values from -0.1875 to 0.1875
- latent_proj: bfloat16 [4096, 4096], P('bytes', 'dp'), may hold values from -0.09375 to 0.09375
- latent_cotangent: bfloat16 [2, 192, 4096], P('dp', 'bytes'), may hold values from -6 to 6
Outputs:
- latent_out: bfloat16 [2, 192, 4096], P('dp', 'bytes')
- pooled_grad: bfloat16 [2, 192, 1024], P('dp', 'bytes')
The draws below stay inside these ranges and needn't reach their ends.
Inputs may be any that keep to these rules, and one draw needn't show every extreme that they name: `patch_starts`: per shard the first entry is 0, entries increase strictly while below 128 and the rest equal 128; a shard has 6 to 12 patches, and in every stream some shard has exactly 12.
All inputs are finite; a program needn't handle non-finite values.
Results may differ from the reference program's by a relative error of at most 0.025.
Values may be sent and summed in bfloat16 or wider, within the bound.
A program may use at most 64 MiB of HBM per device.

```python
import jax
import jax.numpy as jnp
from jax import lax

DL = 1024
HEAD_L = 64
D = 4096
B_DEV = 128
HEADS_L = 16
PCAP = 12
WIN = 256
STREAMS = 2
SEQ = 2048
PATCHES = 192
N_BYTES = 16


def key_jitter(key):
    return jnp.clip(jax.random.normal(jax.random.fold_in(key, 11), (STREAMS, SEQ, DL), jnp.float32), -6.0, 6.0)


def draw_byte_keys(key, part):
    base = key_jitter(key)
    return base.astype(jnp.bfloat16)


def draw_byte_queries(key, part):
    return jnp.clip(jax.random.normal(jax.random.fold_in(key, 13), (STREAMS, SEQ, DL), jnp.float32), -6.0, 6.0).astype(jnp.bfloat16)


def draw_patch_starts(key, part):
    base = jax.random.fold_in(key, 3)
    first_key, count_key, order_key = jax.random.split(base, 3)
    full = jax.random.randint(first_key, (STREAMS, 1), 0, N_BYTES)
    counts = jax.random.randint(count_key, (STREAMS, N_BYTES), PCAP // 2, PCAP + 1)
    counts = jnp.where(jnp.arange(N_BYTES, dtype=jnp.int32)[None, :] == full, PCAP, counts)
    scores = jax.random.randint(order_key, (STREAMS, N_BYTES, B_DEV - 1), 0, 2 ** 20)
    scores = scores * B_DEV + jnp.arange(B_DEV - 1, dtype=jnp.int32)[None, None, :]
    order = jnp.argsort(scores, axis=-1, stable=True).astype(jnp.int32)
    picks = order[:, :, :PCAP - 1] + 1
    slots = jnp.arange(PCAP - 1, dtype=jnp.int32)[None, None, :]
    picks = jnp.where(slots < counts[:, :, None] - 1, picks, B_DEV)
    picks = jnp.sort(picks, axis=-1)
    zeros = jnp.zeros((STREAMS, N_BYTES, 1), jnp.int32)
    return jnp.concatenate([zeros, picks], axis=-1).astype(jnp.int32)


def block_levels(stream_key, dims, cuts, low, largest):
    factor_of, own = 1.0, jax.random.fold_in(stream_key, 6)
    for position, shards_of in cuts:
        draws = jnp.exp(jax.random.uniform(jax.random.fold_in(own, position), (shards_of,), jnp.float32, low / len(cuts), largest / len(cuts)))
        factor_of = factor_of * jnp.repeat(draws, dims[position] // shards_of).reshape([-1 if axis == position else 1 for axis in range(len(dims))])
    return factor_of


def noise(own_key, dims, spread, most, pieces=(), kind=jnp.bfloat16):
    entries = spread * jax.random.normal(own_key, dims, jnp.float32)
    if pieces:
        entries = entries * block_levels(own_key, dims, pieces, -0.22, 0.18)
    return jnp.clip(entries, -most, most).astype(kind)


def setup_inputs(seed: int = 0) -> dict:
    key_list = jax.random.split(jax.random.key(seed), 8)
    byte_queries = draw_byte_queries(jax.random.fold_in(key_list[7], 71), 0)
    byte_keys = draw_byte_keys(jax.random.fold_in(key_list[7], 71), 0)
    byte_values = noise(key_list[2], (STREAMS, SEQ, DL), 1.0, 6.0, ((0, 2), (1, 16)))
    patch_starts = draw_patch_starts(jax.random.fold_in(key_list[7], 71), 0)
    patch_proj = noise(key_list[4], (DL, D), DL ** -0.5, 0.1875, ((0, 2), (1, 16)))
    latent_proj = noise(key_list[5], (D, D), D ** -0.5, 0.09375, ((0, 16), (1, 2)))
    latent_cotangent = noise(key_list[6], (STREAMS, PATCHES, D), 1.0, 6.0, ((0, 2), (1, 16)))
    return {"byte_queries": byte_queries, "byte_keys": byte_keys, "byte_values": byte_values, "patch_starts": patch_starts, "patch_proj": patch_proj, "latent_proj": latent_proj, "latent_cotangent": latent_cotangent}


def encode(query, keys, values):
    shape = (N_BYTES, B_DEV, HEADS_L, HEAD_L)
    qb = query.reshape(shape).astype(jnp.float32)
    kb = keys.reshape(shape).astype(jnp.float32)
    vb = values.reshape(shape).astype(jnp.float32)
    k_one = jnp.concatenate([jnp.zeros_like(kb[:1]), kb[:-1]], axis=0)
    v_one = jnp.concatenate([jnp.zeros_like(vb[:1]), vb[:-1]], axis=0)
    k_two = jnp.concatenate([jnp.zeros_like(kb[:2]), kb[:-2]], axis=0)
    v_two = jnp.concatenate([jnp.zeros_like(vb[:2]), vb[:-2]], axis=0)
    k_all = jnp.concatenate([k_two, k_one, kb], axis=1)
    v_all = jnp.concatenate([v_two, v_one, vb], axis=1)
    scores = jnp.einsum("nihd,njhd->nhij", qb, k_all) * (HEAD_L ** -0.5)
    qpos = jnp.arange(B_DEV, dtype=jnp.int32)[:, None] + 2 * B_DEV
    kpos = jnp.arange(3 * B_DEV, dtype=jnp.int32)[None, :]
    inside = (kpos <= qpos) & (kpos > qpos - WIN)
    shard = jnp.arange(N_BYTES, dtype=jnp.int32)[:, None, None, None]
    kp = kpos[None, None]
    reach = (kp >= 2 * B_DEV) | ((kp >= B_DEV) & (shard >= 1)) | (shard >= 2)
    allowed = inside[None, None] & reach
    scores = jnp.where(allowed, scores, -1e30)
    top = jnp.max(scores, axis=-1, keepdims=True)
    expo = jnp.exp(scores - top)
    weights = (expo / jnp.sum(expo, axis=-1, keepdims=True)).astype(jnp.bfloat16)
    encoded = jnp.einsum("nhij,njhd->nihd", weights.astype(jnp.float32), v_all)
    return encoded.astype(jnp.bfloat16).reshape(N_BYTES, B_DEV, DL)


def pool(encoded, starts):
    nexts = jnp.concatenate([starts[:, 1:], jnp.full((N_BYTES, 1), B_DEV, jnp.int32)], axis=1)
    place = jnp.arange(B_DEV, dtype=jnp.int32)[None, None, :]
    member = (place >= starts[:, :, None]) & (place < nexts[:, :, None])
    length = jnp.sum(member.astype(jnp.float32), axis=-1)
    summed = jnp.einsum("npb,nbd->npd", member.astype(jnp.float32), encoded.astype(jnp.float32))
    pooled = summed / jnp.maximum(length, 1.0)[..., None]
    return pooled.astype(jnp.bfloat16).reshape(PATCHES, DL)


def one_stream(items, patch_proj, latent_proj):
    query, keys, values, starts, cotangent = items
    pooled = pool(encode(query, keys, values), starts)
    valid = (starts < B_DEV).reshape(PATCHES)
    block = D // N_BYTES
    hidden_in = jnp.dot(pooled, patch_proj, preferred_element_type=jnp.float32)
    activation = jax.nn.silu(hidden_in).astype(jnp.bfloat16)
    activation_tiles = activation.reshape(PATCHES, N_BYTES, block).transpose(1, 0, 2).astype(jnp.float32)
    weight_tiles = latent_proj.reshape(N_BYTES, block, D).astype(jnp.float32)
    part_pieces = jnp.einsum("foy,fyw->fow", activation_tiles, weight_tiles).astype(jnp.bfloat16)
    part_pieces = lax.optimization_barrier(part_pieces).astype(jnp.float32)
    latent_out = jnp.sum(part_pieces, axis=0).astype(jnp.bfloat16)
    back = jnp.dot(cotangent, latent_proj.T, preferred_element_type=jnp.float32)
    sigma = jax.nn.sigmoid(hidden_in)
    act_grad = (back * sigma * (1.0 + hidden_in * (1.0 - sigma))).astype(jnp.bfloat16)
    grad_blocks = act_grad.reshape(PATCHES, N_BYTES, block).transpose(1, 0, 2).astype(jnp.float32)
    proj_blocks = patch_proj.reshape(DL, N_BYTES, block).transpose(1, 0, 2).astype(jnp.float32)
    gparts = jnp.einsum("bpk,bek->bpe", grad_blocks, proj_blocks).astype(jnp.bfloat16)
    gparts = lax.optimization_barrier(gparts).astype(jnp.float32)
    pooled_grad = jnp.where(valid[:, None], jnp.sum(gparts, axis=0), 0.0).astype(jnp.bfloat16)
    return latent_out, pooled_grad


def reference(byte_queries, byte_keys, byte_values, patch_starts, patch_proj, latent_proj, latent_cotangent):
    def step(items):
        return one_stream(items, patch_proj, latent_proj)

    latent_out, pooled_grad = lax.map(step, (byte_queries, byte_keys, byte_values, patch_starts, latent_cotangent))
    return latent_out, pooled_grad
```

```python
import functools

import jax
import jax.numpy as jnp
from jax import lax
from jax.experimental import pallas as pl
from jax.experimental.pallas import tpu as pltpu
from jax.sharding import PartitionSpec as P

HEAD_L = 64
MESH = pl.DeviceIdType.MESH
SLAB = 16
F32 = jnp.float32
BF16 = jnp.bfloat16
NT = (((1,), (1,)), ((), ()))


def remote(src, dst, send, recv, target):
    return pltpu.make_async_remote_copy(
        src_ref=src, dst_ref=dst, send_sem=send, recv_sem=recv, device_id=target, device_id_type=MESH
    )


def kernel(
    n,
    exchange,
    starts_ref,
    q_ref,
    k_ref,
    v_ref,
    cot_ref,
    pp_ref,
    lp_ref,
    latent_ref,
    grad_ref,
    kbuf,
    vbuf,
    enc,
    pool,
    cots,
    pp,
    lp,
    act,
    own,
    sib_out,
    sib_in,
    y_out,
    y_in,
    z_out,
    z_in,
    loc_sem,
    wsend,
    wrecv,
    ksend,
    krecv,
    ssend,
    srecv,
    pzs,
    pzr,
    pfs,
    pfr,
    czs,
    czr,
    cfs,
    cfr,
    rss,
    rsr,
    rys,
    ryr,
    rzs,
    rzr,
):
    rows, width = q_ref.shape
    d = lax.axis_index("dp")
    b = lax.axis_index("bytes")
    nz = n // 4
    chips = n // 2
    chip = b // 2
    core = b % 2
    y = chip % 2
    z = chip // 2
    groups = kbuf.shape[2] // 256
    chunks = own.shape[0]
    lat_chunks = chunks - 1
    cw = own.shape[2]
    slots = latent_ref.shape[0]
    half = n // 2 * SLAB
    quarter = half // 2

    sibling = {"bytes": chip * 2 + 1 - core}
    y_peer = {"bytes": (z * 2 + 1 - y) * 2 + core}
    onward = {"bytes": lax.rem(chip + 1, chips) * 2 + core}
    other = jnp.where(y == 1, lax.rem(chip + 1, chips), lax.rem(chip + chips - 1, chips))

    def z_peer(j):
        return {"bytes": (lax.rem(z + j, nz) * 2 + y) * 2 + core}

    def slab(zz):
        return pl.ds(pl.multiple_of(((core * 2 + y) * nz + zz) * SLAB, SLAB), SLAB)

    y_half = pl.ds(pl.multiple_of((core * 2 + y) * quarter, SLAB), quarter)
    y_half_in = pl.ds(pl.multiple_of((core * 2 + 1 - y) * quarter, SLAB), quarter)
    c_half = pl.ds(pl.multiple_of(core * half, SLAB), half)
    c_half_in = pl.ds(pl.multiple_of((1 - core) * half, SLAB), half)

    if exchange:
        p_rows, l_cols = pp_ref.shape[0], lp_ref.shape[1]
        p_own = pl.ds(pl.multiple_of(d * p_rows, 256), p_rows)
        p_got = pl.ds(pl.multiple_of((1 - d) * p_rows, 256), p_rows)
        l_own = pl.ds(pl.multiple_of(d * l_cols, 256), l_cols)
        l_got = pl.ds(pl.multiple_of((1 - d) * l_cols, 256), l_cols)
        partner = {"dp": 1 - d}
        p_local = pltpu.make_async_copy(pp_ref, pp.at[p_own], loc_sem.at[0])
        l_local = pltpu.make_async_copy(lp_ref, lp.at[:, l_own], loc_sem.at[1])
    else:
        p_local = pltpu.make_async_copy(pp_ref, pp, loc_sem.at[0])
        l_local = pltpu.make_async_copy(lp_ref, lp, loc_sem.at[1])

    barrier = pltpu.get_barrier_semaphore()
    greeted = [sibling, y_peer, {"bytes": other * 2 + core}] + [z_peer(j) for j in range(1, nz)]
    if exchange:
        greeted.append(partner)
    for device in greeted:
        pl.semaphore_signal(barrier, inc=1, device_id=device, device_id_type=MESH)
    p_local.start()
    l_local.start()
    my_slab = slab(z)
    cots[my_slab, :] = jnp.zeros((SLAB, cots.shape[1]), BF16)
    cots[pl.ds(pl.multiple_of(((core * 2 + y) * nz + z) * SLAB, SLAB), slots), :] = cot_ref[...]
    pl.semaphore_wait(barrier, len(greeted))

    def cols(g):
        return pl.ds(pl.multiple_of(g * 256, 256), 256)

    def ahead(t, g):
        ref, buf = ((k_ref, kbuf), (v_ref, vbuf))[t]
        return remote(ref.at[:, cols(g)], buf.at[0, :, cols(g)], ksend.at[t, g], krecv.at[t, g], onward)

    def across(t, g):
        ref, buf = ((k_ref, kbuf), (v_ref, vbuf))[t]
        return remote(ref.at[:, cols(g)], buf.at[1, :, cols(g)], ssend.at[t, g], srecv.at[t, g], sibling)

    def passed(t, g):
        buf = (kbuf, vbuf)[t]
        return remote(buf.at[0, :, cols(g)], buf.at[1, :, cols(g)], ssend.at[t, g], srecv.at[t, g], sibling)

    @pl.when(chip < chips - 1)
    def _():
        @pl.loop(0, groups)
        def _(g):
            ahead(0, g).start()
            ahead(1, g).start()

    @pl.when(core == 0)
    def _():
        @pl.loop(0, groups)
        def _(g):
            across(0, g).start()
            across(1, g).start()

    if exchange:
        p_remote = remote(pp_ref, pp.at[p_own], wsend.at[0], wrecv.at[0], partner)
        l_remote = remote(lp_ref, lp.at[:, l_own], wsend.at[1], wrecv.at[1], partner)
        p_remote.start()
        l_remote.start()
    cot_z = [
        remote(cots.at[my_slab], cots.at[my_slab], czs.at[j - 1], czr.at[j - 1], z_peer(j))
        for j in range(1, nz)
    ]
    for copy in cot_z:
        copy.start()

    @pl.when(chip == 0)
    def _():
        kbuf[0] = jnp.zeros((rows, width), BF16)
        vbuf[0] = jnp.zeros((rows, width), BF16)

    @pl.when(b == 0)
    def _():
        kbuf[1] = jnp.zeros((rows, width), BF16)
        vbuf[1] = jnp.zeros((rows, width), BF16)

    slot_row = lax.broadcasted_iota(jnp.int32, (SLAB, rows), 0)
    place = lax.broadcasted_iota(jnp.int32, (SLAB, rows), 1)
    first = jnp.full((SLAB, rows), rows, jnp.int32)
    last = jnp.full((SLAB, rows), rows, jnp.int32)
    for p in range(slots):
        first = jnp.where(slot_row == p, starts_ref[0, p], first)
        if p + 1 < slots:
            last = jnp.where(slot_row == p, starts_ref[0, p + 1], last)
    member = jnp.where((place >= first) & (place < last), 1.0, 0.0).astype(F32)
    length = jnp.maximum(jnp.sum(member, axis=1, keepdims=True), 1.0)
    member = member.astype(BF16)
    valid = jnp.max(first, axis=1, keepdims=True) < rows

    lane = lax.broadcasted_iota(jnp.int32, (rows, 128), 1)
    query_row = lax.broadcasted_iota(jnp.int32, (2 * rows, rows), 0)
    query_row = jnp.where(query_row >= rows, query_row - rows, query_row)
    causal = lax.broadcasted_iota(jnp.int32, (2 * rows, rows), 1) <= query_row
    low = lane < HEAD_L
    far_bias = jnp.where(chip >= 1, 0.0, -1e30).astype(F32)
    mid_bias = jnp.where(b >= 1, 0.0, -1e30).astype(F32)

    def await_group(t, g):
        @pl.when(chip >= 1)
        def _():
            ahead(t, g).wait_recv()

        @pl.when((core == 1) & (chip >= 1))
        def _():
            passed(t, g).start()

        @pl.when((core == 1) | (chip >= 1))
        def _():
            across(t, g).wait_recv()

    @pl.loop(0, groups)
    def _(g):
        await_group(0, g)
        await_group(1, g)

        for pair in range(2):
            at = pl.ds(pl.multiple_of(g * 256 + pair * 128, 128), 128)
            q = q_ref[:, at].astype(F32) * HEAD_L ** (-0.5)
            q2 = jnp.concatenate([jnp.where(low, q, 0.0), jnp.where(low, 0.0, q)], axis=0).astype(BF16)
            s_own = lax.dot_general(q2, k_ref[:, at], NT, preferred_element_type=F32)
            s_mid = lax.dot_general(q2, kbuf[1, :, at], NT, preferred_element_type=F32) + mid_bias
            s_far = lax.dot_general(q2, kbuf[0, :, at], NT, preferred_element_type=F32) + far_bias
            s_two = jnp.where(causal, s_own, s_far)
            top = jnp.max(jnp.maximum(s_two, s_mid), axis=1, keepdims=True)
            e_two = jnp.exp(s_two - top)
            e_mid = jnp.exp(s_mid - top)
            total = jnp.sum(e_two + e_mid, axis=1, keepdims=True)
            e_own = jnp.where(causal, e_two, 0.0).astype(BF16)
            e_far = jnp.where(causal, 0.0, e_two).astype(BF16)
            mixed = jnp.dot(e_own, v_ref[:, at], preferred_element_type=F32)
            mixed += jnp.dot(e_mid.astype(BF16), vbuf[1, :, at], preferred_element_type=F32)
            mixed += jnp.dot(e_far, vbuf[0, :, at], preferred_element_type=F32)
            mixed = mixed / total
            enc[:, at] = jnp.where(low, mixed[:rows], mixed[rows:]).astype(BF16)
        summed = jnp.dot(member, enc[:, cols(g)], preferred_element_type=F32)
        pool[my_slab, cols(g)] = (summed / length).astype(BF16)

    pool_z = [
        remote(pool.at[my_slab], pool.at[my_slab], pzs.at[j - 1], pzr.at[j - 1], z_peer(j))
        for j in range(1, nz)
    ]
    for copy in pool_z:
        copy.start()
    cot_y = remote(cots.at[y_half], cots.at[y_half], cfs.at[0], cfr.at[0], y_peer)
    cot_c = remote(cots.at[c_half], cots.at[c_half], cfs.at[1], cfr.at[1], sibling)
    pool_y = remote(pool.at[y_half], pool.at[y_half], pfs.at[0], pfr.at[0], y_peer)
    pool_c = remote(pool.at[c_half], pool.at[c_half], pfs.at[1], pfr.at[1], sibling)

    def await_z(buf, sends, recvs):
        for j in range(1, nz):
            from_slab = slab(lax.rem(z + nz - j, nz))
            remote(buf.at[from_slab], buf.at[from_slab], sends.at[j - 1], recvs.at[j - 1], z_peer(j)).wait_recv()

    await_z(pool, pzs, pzr)
    pool_y.start()
    await_z(cots, czs, czr)
    cot_y.start()
    remote(pool.at[y_half_in], pool.at[y_half_in], pfs.at[0], pfr.at[0], y_peer).wait_recv()
    pool_c.start()
    remote(pool.at[c_half_in], pool.at[c_half_in], pfs.at[1], pfr.at[1], sibling).wait_recv()

    p_local.wait()
    if exchange:
        remote(pp_ref, pp.at[p_got], wsend.at[0], wrecv.at[0], partner).wait_recv()
    hidden = jnp.dot(pool[...], pp[...], preferred_element_type=F32)
    sigma = 1.0 / (1.0 + jnp.exp(-hidden))
    act[...] = (hidden * sigma).astype(BF16)
    slope = sigma * (1.0 + hidden * (1.0 - sigma))

    l_local.wait()
    if exchange:
        remote(lp_ref, lp.at[:, l_got], wsend.at[1], wrecv.at[1], partner).wait_recv()

    mine = pl.ds(pl.multiple_of(core * half, SLAB), half)
    theirs = pl.ds(pl.multiple_of((1 - core) * half, SLAB), half)

    def to_sibling(c):
        return remote(sib_out.at[c], sib_in.at[c], rss.at[c], rsr.at[c], sibling)

    def to_y(c):
        return remote(y_out.at[c], y_in.at[c], rys.at[c], ryr.at[c], y_peer)

    def to_z(c, j):
        return remote(z_out.at[c, j - 1], z_in.at[c, j - 1], rzs.at[c, j - 1], rzr.at[c, j - 1], z_peer(j))

    def c_cols(c):
        return pl.ds(pl.multiple_of(c * cw, 128), cw)

    @pl.loop(0, lat_chunks)
    def _(c):
        w = lp[:, c_cols(c)]
        sib_out[c] = jnp.dot(act[theirs, :], w, preferred_element_type=F32).astype(BF16)
        to_sibling(c).start()
        own[c] = jnp.dot(act[mine, :], w, preferred_element_type=F32)

    remote(cots.at[y_half_in], cots.at[y_half_in], cfs.at[0], cfr.at[0], y_peer).wait_recv()
    cot_c.start()

    def y_step(c):
        to_sibling(c).wait_recv()
        there = pl.ds(pl.multiple_of((1 - y) * quarter, SLAB), quarter)
        here = pl.ds(pl.multiple_of(y * quarter, SLAB), quarter)
        y_out[c] = (own[c, there, :] + sib_in[c, there, :].astype(F32)).astype(BF16)
        to_y(c).start()
        own[c, here, :] = own[c, here, :] + sib_in[c, here, :].astype(F32)

    def z_step(c):
        to_y(c).wait_recv()
        for j in range(1, nz):
            zz = lax.rem(z + j, nz)
            at = pl.ds(pl.multiple_of(y * quarter + zz * SLAB, SLAB), SLAB)
            got = pl.ds(pl.multiple_of(zz * SLAB, SLAB), SLAB)
            z_out[c, j - 1] = (own[c, at, :] + y_in[c, got, :].astype(F32)).astype(BF16)
            to_z(c, j).start()

    def last_step(c):
        at = pl.ds(pl.multiple_of(y * quarter + z * SLAB, SLAB), SLAB)
        got = pl.ds(pl.multiple_of(z * SLAB, SLAB), SLAB)
        total = own[c, at, :] + y_in[c, got, :].astype(F32)
        for j in range(1, nz):
            to_z(c, j).wait_recv()
            total = total + z_in[c, j - 1].astype(F32)
        return total

    pl.loop(0, lat_chunks)(y_step)

    remote(cots.at[c_half_in], cots.at[c_half_in], cfs.at[1], cfr.at[1], sibling).wait_recv()
    back = lax.dot_general(cots[...], lp[...], NT, preferred_element_type=F32)
    act[...] = (back * slope).astype(BF16)
    g = lat_chunks
    sib_out[g] = lax.dot_general(act[theirs, :], pp[...], NT, preferred_element_type=F32).astype(BF16)
    to_sibling(g).start()
    own[g] = lax.dot_general(act[mine, :], pp[...], NT, preferred_element_type=F32)
    y_step(g)

    pl.loop(0, chunks)(z_step)

    @pl.loop(0, lat_chunks)
    def _(c):
        latent_ref[:, c_cols(c)] = last_step(c)[:slots].astype(BF16)

    grad_ref[...] = jnp.where(valid, last_step(g), 0.0)[:slots].astype(BF16)

    @pl.when(chip < chips - 1)
    def _():
        @pl.loop(0, groups)
        def _(g):
            ahead(0, g).wait_send()
            ahead(1, g).wait_send()

    @pl.when((core == 0) | (chip >= 1))
    def _():
        @pl.loop(0, groups)
        def _(g):
            across(0, g).wait_send()
            across(1, g).wait_send()

    if exchange:
        p_remote.wait_send()
        l_remote.wait_send()
    for copy in cot_z + pool_z + [cot_y, cot_c, pool_y, pool_c]:
        copy.wait_send()

    @pl.loop(0, chunks)
    def _(c):
        to_sibling(c).wait_send()
        to_y(c).wait_send()
        for j in range(1, nz):
            to_z(c, j).wait_send()


def per_device(
    n,
    exchange,
    byte_queries,
    byte_keys,
    byte_values,
    patch_starts,
    patch_proj,
    latent_proj,
    latent_cotangent,
):
    rows, width = byte_queries.shape[1:]
    slots, wide = latent_cotangent.shape[1:]
    if not exchange:
        patch_proj = lax.all_gather(patch_proj, "dp", axis=0, tiled=True)
        latent_proj = lax.all_gather(latent_proj, "dp", axis=1, tiled=True)
    block = patch_proj.shape[1]
    nz = n // 4
    cw = width
    chunks = wide // cw + 1
    groups = width // 256
    half = n // 2 * SLAB
    vmem = pl.BlockSpec(memory_space=pltpu.VMEM)
    hbm = pl.BlockSpec(memory_space=pl.ANY)
    dma = pltpu.SemaphoreType.DMA
    latent, grads = pl.pallas_call(
        functools.partial(kernel, n, exchange),
        out_shape=(
            jax.ShapeDtypeStruct((slots, wide), BF16),
            jax.ShapeDtypeStruct((slots, width), BF16),
        ),
        in_specs=[pl.BlockSpec(memory_space=pltpu.SMEM), vmem, vmem, vmem, vmem, hbm, hbm],
        out_specs=(vmem, vmem),
        scratch_shapes=[
            pltpu.VMEM((2, rows, width), BF16),
            pltpu.VMEM((2, rows, width), BF16),
            pltpu.VMEM((rows, width), BF16),
            pltpu.VMEM((n * SLAB, width), BF16),
            pltpu.VMEM((n * SLAB, wide), BF16),
            pltpu.VMEM((width, block), BF16),
            pltpu.VMEM((block, wide), BF16),
            pltpu.VMEM((n * SLAB, block), BF16),
            pltpu.VMEM((chunks, half, cw), F32),
            pltpu.VMEM((chunks, half, cw), BF16),
            pltpu.VMEM((chunks, half, cw), BF16),
            pltpu.VMEM((chunks, half // 2, cw), BF16),
            pltpu.VMEM((chunks, half // 2, cw), BF16),
            pltpu.VMEM((chunks, nz - 1, SLAB, cw), BF16),
            pltpu.VMEM((chunks, nz - 1, SLAB, cw), BF16),
            dma((2,)),
            dma((2,)),
            dma((2,)),
            dma((2, groups)),
            dma((2, groups)),
            dma((2, groups)),
            dma((2, groups)),
            dma((nz - 1,)),
            dma((nz - 1,)),
            dma((2,)),
            dma((2,)),
            dma((nz - 1,)),
            dma((nz - 1,)),
            dma((2,)),
            dma((2,)),
            dma((chunks,)),
            dma((chunks,)),
            dma((chunks,)),
            dma((chunks,)),
            dma((chunks, nz - 1)),
            dma((chunks, nz - 1)),
        ],
        compiler_params=pltpu.CompilerParams(
            collective_id=0, has_side_effects=True, vmem_limit_bytes=44 * 2**20
        ),
        cost_estimate=pl.CostEstimate(flops=2 * 10**9, bytes_accessed=4 * 10**6, transcendentals=10**6),
    )(
        patch_starts[0],
        byte_queries[0],
        byte_keys[0],
        byte_values[0],
        latent_cotangent[0],
        patch_proj,
        latent_proj,
    )
    return latent[None], grads[None]


def solution(mesh):
    n = mesh.shape["bytes"]
    return jax.shard_map(
        functools.partial(per_device, n, mesh.shape["dp"] == 2),
        mesh=mesh,
        in_specs=(
            P("dp", "bytes", None),
            P("dp", "bytes", None),
            P("dp", "bytes", None),
            P("dp", "bytes", None),
            P("dp", "bytes"),
            P("bytes", "dp"),
            P("dp", "bytes", None),
        ),
        out_specs=(P("dp", "bytes", None), P("dp", "bytes", None)),
        check_vma=False,
    )
```

```python
import functools

import jax
import jax.numpy as jnp
from jax import lax
from jax.experimental import pallas as pl
from jax.experimental.pallas import tpu as pltpu
from jax.sharding import PartitionSpec as P

HEAD_L = 64
MESH = pl.DeviceIdType.MESH
SLAB = 16
F32 = jnp.float32
BF16 = jnp.bfloat16
NT = (((1,), (1,)), ((), ()))


def remote(src, dst, send, recv, target):
    return pltpu.make_async_remote_copy(
        src_ref=src, dst_ref=dst, send_sem=send, recv_sem=recv, device_id=target, device_id_type=MESH
    )


def kernel(
    n,
    exchange,
    starts_hbm,
    q_hbm,
    k_hbm,
    v_hbm,
    cot_hbm,
    pp_ref,
    lp_ref,
    latent_ref,
    grad_ref,
    starts_ref,
    q_ref,
    k_ref,
    v_ref,
    cot_ref,
    kbuf,
    vbuf,
    enc,
    pool,
    cots,
    pp,
    lp,
    act,
    own,
    sib_out,
    sib_in,
    y_out,
    y_in,
    z_out,
    z_in,
    in_sem,
    loc_sem,
    wsend,
    wrecv,
    ksend,
    krecv,
    ssend,
    srecv,
    pzs,
    pzr,
    pfs,
    pfr,
    czs,
    czr,
    cfs,
    cfr,
    rss,
    rsr,
    rys,
    ryr,
    rzs,
    rzr,
):
    rows, width = q_ref.shape
    d = lax.axis_index("dp")
    b = lax.axis_index("bytes")
    nz = n // 4
    chips = n // 2
    chip = b // 2
    core = b % 2
    y = chip % 2
    z = chip // 2
    groups = kbuf.shape[2] // 256
    chunks = own.shape[0]
    lat_chunks = chunks - 1
    cw = own.shape[2]
    slots = latent_ref.shape[0]
    half = n // 2 * SLAB
    quarter = half // 2
    tight = n // 2 * slots

    sibling = {"bytes": chip * 2 + 1 - core}
    y_peer = {"bytes": (z * 2 + 1 - y) * 2 + core}
    onward = {"bytes": lax.rem(chip + 1, chips) * 2 + core}
    other = jnp.where(y == 1, lax.rem(chip + 1, chips), lax.rem(chip + chips - 1, chips))

    def z_peer(j):
        return {"bytes": (lax.rem(z + j, nz) * 2 + y) * 2 + core}

    def slab(zz):
        return pl.ds(pl.multiple_of(((core * 2 + y) * nz + zz) * SLAB, SLAB), SLAB)

    y_half = pl.ds(pl.multiple_of((core * 2 + y) * quarter, SLAB), quarter)
    y_half_in = pl.ds(pl.multiple_of((core * 2 + 1 - y) * quarter, SLAB), quarter)
    c_half = pl.ds(pl.multiple_of(core * half, SLAB), half)
    c_half_in = pl.ds(pl.multiple_of((1 - core) * half, SLAB), half)

    if exchange:
        p_rows, l_cols = pp_ref.shape[0], lp_ref.shape[1]
        p_own = pl.ds(pl.multiple_of(d * p_rows, 256), p_rows)
        p_got = pl.ds(pl.multiple_of((1 - d) * p_rows, 256), p_rows)
        l_own = pl.ds(pl.multiple_of(d * l_cols, 256), l_cols)
        l_got = pl.ds(pl.multiple_of((1 - d) * l_cols, 256), l_cols)
        partner = {"dp": 1 - d}
        p_local = pltpu.make_async_copy(pp_ref, pp.at[p_own], loc_sem.at[0])
        l_local = pltpu.make_async_copy(lp_ref, lp.at[:, l_own], loc_sem.at[1])
    else:
        p_local = pltpu.make_async_copy(pp_ref, pp, loc_sem.at[0])
        l_local = pltpu.make_async_copy(lp_ref, lp, loc_sem.at[1])

    loads = [
        pltpu.make_async_copy(src, dst, in_sem.at[i])
        for i, (src, dst) in enumerate(
            (
                (cot_hbm, cot_ref),
                (starts_hbm, starts_ref),
                (q_hbm, q_ref),
                (k_hbm, k_ref),
                (v_hbm, v_ref),
            )
        )
    ]
    barrier = pltpu.get_barrier_semaphore()
    greeted = [sibling, y_peer, {"bytes": other * 2 + core}] + [z_peer(j) for j in range(1, nz)]
    if exchange:
        greeted.append(partner)
    for device in greeted:
        pl.semaphore_signal(barrier, inc=1, device_id=device, device_id_type=MESH)
    for copy in loads:
        copy.start()
    my_slab = slab(z)
    cots[my_slab, :] = jnp.zeros((SLAB, cots.shape[1]), BF16)
    loads[0].wait()
    cots[pl.ds(pl.multiple_of(((core * 2 + y) * nz + z) * SLAB, SLAB), slots), :] = cot_ref[...]
    pl.semaphore_wait(barrier, len(greeted))

    def cols(g):
        return pl.ds(pl.multiple_of(g * 256, 256), 256)

    def ahead(t, g):
        ref, buf = ((k_hbm, kbuf), (v_hbm, vbuf))[t]
        return remote(ref.at[:, cols(g)], buf.at[0, :, cols(g)], ksend.at[t, g], krecv.at[t, g], onward)

    def across(t, g):
        ref, buf = ((k_hbm, kbuf), (v_hbm, vbuf))[t]
        return remote(ref.at[:, cols(g)], buf.at[1, :, cols(g)], ssend.at[t, g], srecv.at[t, g], sibling)

    def passed(t, g):
        buf = (kbuf, vbuf)[t]
        return remote(buf.at[0, :, cols(g)], buf.at[1, :, cols(g)], ssend.at[t, g], srecv.at[t, g], sibling)

    @pl.when(chip < chips - 1)
    def _():
        @pl.loop(0, groups)
        def _(g):
            ahead(0, g).start()
            ahead(1, g).start()

    @pl.when(core == 0)
    def _():
        @pl.loop(0, groups)
        def _(g):
            across(0, g).start()
            across(1, g).start()

    if exchange:
        p_remote = remote(pp_ref, pp.at[p_own], wsend.at[0], wrecv.at[0], partner)
        l_remote = remote(lp_ref, lp.at[:, l_own], wsend.at[1], wrecv.at[1], partner)
        p_remote.start()
        l_remote.start()
    cot_z = [
        remote(cots.at[my_slab], cots.at[my_slab], czs.at[j - 1], czr.at[j - 1], z_peer(j))
        for j in range(1, nz)
    ]
    for copy in cot_z:
        copy.start()
    p_local.start()
    l_local.start()

    @pl.when(chip == 0)
    def _():
        kbuf[0] = jnp.zeros((rows, width), BF16)
        vbuf[0] = jnp.zeros((rows, width), BF16)

    @pl.when(b == 0)
    def _():
        kbuf[1] = jnp.zeros((rows, width), BF16)
        vbuf[1] = jnp.zeros((rows, width), BF16)

    loads[1].wait()
    slot_row = lax.broadcasted_iota(jnp.int32, (SLAB, rows), 0)
    place = lax.broadcasted_iota(jnp.int32, (SLAB, rows), 1)
    first = jnp.full((SLAB, rows), rows, jnp.int32)
    last = jnp.full((SLAB, rows), rows, jnp.int32)
    for p in range(slots):
        first = jnp.where(slot_row == p, starts_ref[0, p], first)
        if p + 1 < slots:
            last = jnp.where(slot_row == p, starts_ref[0, p + 1], last)
    member = jnp.where((place >= first) & (place < last), 1.0, 0.0).astype(F32)
    length = jnp.maximum(jnp.sum(member, axis=1, keepdims=True), 1.0)
    member = member.astype(BF16)
    valid = jnp.max(first, axis=1, keepdims=True) < rows

    lane = lax.broadcasted_iota(jnp.int32, (rows, 128), 1)
    query_row = lax.broadcasted_iota(jnp.int32, (2 * rows, rows), 0)
    query_row = jnp.where(query_row >= rows, query_row - rows, query_row)
    causal = lax.broadcasted_iota(jnp.int32, (2 * rows, rows), 1) <= query_row
    low = lane < HEAD_L
    far_bias = jnp.where(chip >= 1, 0.0, -1e30).astype(F32)
    mid_bias = jnp.where(b >= 1, 0.0, -1e30).astype(F32)

    def await_group(t, g):
        @pl.when(chip >= 1)
        def _():
            ahead(t, g).wait_recv()

        @pl.when((core == 1) & (chip >= 1))
        def _():
            passed(t, g).start()

        @pl.when((core == 1) | (chip >= 1))
        def _():
            across(t, g).wait_recv()

    cot_y = remote(cots.at[y_half], cots.at[y_half], cfs.at[0], cfr.at[0], y_peer)
    cot_c = remote(cots.at[c_half], cots.at[c_half], cfs.at[1], cfr.at[1], sibling)

    def await_z(buf, sends, recvs):
        for j in range(1, nz):
            from_slab = slab(lax.rem(z + nz - j, nz))
            remote(buf.at[from_slab], buf.at[from_slab], sends.at[j - 1], recvs.at[j - 1], z_peer(j)).wait_recv()

    for copy in loads[2:]:
        copy.wait()

    @pl.loop(0, groups)
    def _(g):
        await_group(0, g)
        await_group(1, g)

        @pl.when(g == groups - 1)
        def _():
            await_z(cots, czs, czr)
            cot_y.start()

        for pair in range(2):
            at = pl.ds(pl.multiple_of(g * 256 + pair * 128, 128), 128)
            q = q_ref[:, at].astype(F32) * HEAD_L ** (-0.5)
            q2 = jnp.concatenate([jnp.where(low, q, 0.0), jnp.where(low, 0.0, q)], axis=0).astype(BF16)
            s_own = lax.dot_general(q2, k_ref[:, at], NT, preferred_element_type=F32)
            s_mid = lax.dot_general(q2, kbuf[1, :, at], NT, preferred_element_type=F32) + mid_bias
            s_far = lax.dot_general(q2, kbuf[0, :, at], NT, preferred_element_type=F32) + far_bias
            s_two = jnp.where(causal, s_own, s_far)
            top = jnp.max(jnp.maximum(s_two, s_mid), axis=1, keepdims=True)
            e_two = jnp.exp(s_two - top)
            e_mid = jnp.exp(s_mid - top)
            total = jnp.sum(e_two + e_mid, axis=1, keepdims=True)
            e_own = jnp.where(causal, e_two, 0.0).astype(BF16)
            e_far = jnp.where(causal, 0.0, e_two).astype(BF16)
            mixed = jnp.dot(e_own, v_ref[:, at], preferred_element_type=F32)
            mixed += jnp.dot(e_mid.astype(BF16), vbuf[1, :, at], preferred_element_type=F32)
            mixed += jnp.dot(e_far, vbuf[0, :, at], preferred_element_type=F32)
            mixed = mixed / total
            enc[:, at] = jnp.where(low, mixed[:rows], mixed[rows:]).astype(BF16)
        summed = jnp.dot(member, enc[:, cols(g)], preferred_element_type=F32)
        pool[my_slab, cols(g)] = (summed / length).astype(BF16)

    pool_z = [
        remote(pool.at[my_slab], pool.at[my_slab], pzs.at[j - 1], pzr.at[j - 1], z_peer(j))
        for j in range(1, nz)
    ]
    for copy in pool_z:
        copy.start()
    pool_y = remote(pool.at[y_half], pool.at[y_half], pfs.at[0], pfr.at[0], y_peer)
    pool_c = remote(pool.at[c_half], pool.at[c_half], pfs.at[1], pfr.at[1], sibling)

    await_z(pool, pzs, pzr)
    pool_y.start()
    remote(pool.at[y_half_in], pool.at[y_half_in], pfs.at[0], pfr.at[0], y_peer).wait_recv()
    pool_c.start()
    remote(pool.at[c_half_in], pool.at[c_half_in], pfs.at[1], pfr.at[1], sibling).wait_recv()

    p_local.wait()
    if exchange:
        remote(pp_ref, pp.at[p_got], wsend.at[0], wrecv.at[0], partner).wait_recv()
    hidden = jnp.dot(pool[...], pp[...], preferred_element_type=F32)
    sigma = 1.0 / (1.0 + jnp.exp(-hidden))
    wide_col = lax.broadcasted_iota(jnp.int32, (n * slots, n * SLAB), 1)
    squeeze = (wide_col >> 4) * slots + (wide_col & 15) == lax.broadcasted_iota(
        jnp.int32, (n * slots, n * SLAB), 0
    )
    squeeze = jnp.where(squeeze & ((wide_col & 15) < slots), 1.0, 0.0).astype(BF16)
    wide_row = lax.broadcasted_iota(jnp.int32, (nz * SLAB, nz * slots), 0)
    spread = (wide_row >> 4) * slots + (wide_row & 15) == lax.broadcasted_iota(
        jnp.int32, (nz * SLAB, nz * slots), 1
    )
    spread = jnp.where(spread & ((wide_row & 15) < slots), 1.0, 0.0).astype(BF16)
    activation = (hidden * sigma).astype(BF16)
    act[...] = jnp.dot(squeeze, activation, preferred_element_type=F32).astype(BF16)
    slope = sigma * (1.0 + hidden * (1.0 - sigma))

    l_local.wait()

    mine = pl.ds(pl.multiple_of(core * tight, SLAB), tight)
    theirs = pl.ds(pl.multiple_of((1 - core) * tight, SLAB), tight)

    def to_sibling(c):
        return remote(sib_out.at[c], sib_in.at[c], rss.at[c], rsr.at[c], sibling)

    def to_y(c):
        return remote(y_out.at[c], y_in.at[c], rys.at[c], ryr.at[c], y_peer)

    def to_z(c, j):
        there = pl.ds(pl.multiple_of(lax.rem(z + j, nz) * SLAB, SLAB), SLAB)
        return remote(z_out.at[c, there], z_in.at[c, j - 1], rzs.at[c, j - 1], rzr.at[c, j - 1], z_peer(j))

    def c_cols(c):
        if exchange:
            c = lax.rem(c + d * (lat_chunks // 2), lat_chunks)
        return pl.ds(pl.multiple_of(c * cw, 128), cw)

    def product(c):
        w = lp[:, c_cols(c)]
        sib_out[c] = jnp.dot(act[theirs, :], w, preferred_element_type=F32).astype(BF16)
        to_sibling(c).start()
        own[c] = jnp.dot(act[mine, :], w, preferred_element_type=F32)

    pl.loop(0, lat_chunks // 2)(product)
    if exchange:
        remote(lp_ref, lp.at[:, l_got], wsend.at[1], wrecv.at[1], partner).wait_recv()
    pl.loop(lat_chunks // 2, lat_chunks)(product)

    remote(cots.at[y_half_in], cots.at[y_half_in], cfs.at[0], cfr.at[0], y_peer).wait_recv()
    cot_c.start()

    def y_step(c):
        to_sibling(c).wait_recv()
        there = pl.ds(pl.multiple_of((1 - y) * (tight // 2), SLAB), tight // 2)
        here = pl.ds(pl.multiple_of(y * (tight // 2), SLAB), tight // 2)
        y_out[c] = (own[c, there, :] + sib_in[c, there, :].astype(F32)).astype(BF16)
        to_y(c).start()
        own[c, here, :] = own[c, here, :] + sib_in[c, here, :].astype(F32)

    def z_step(c):
        to_y(c).wait_recv()
        here = pl.ds(pl.multiple_of(y * (tight // 2), SLAB), tight // 2)
        total = (own[c, here, :] + y_in[c].astype(F32)).astype(BF16)
        z_out[c] = jnp.dot(spread, total, preferred_element_type=F32).astype(BF16)
        for j in range(1, nz):
            to_z(c, j).start()

    def last_step(c):
        total = z_out[c, pl.ds(pl.multiple_of(z * SLAB, SLAB), SLAB), :].astype(F32)
        for j in range(1, nz):
            to_z(c, j).wait_recv()
            total = total + z_in[c, j - 1].astype(F32)
        return total

    pl.loop(0, lat_chunks)(y_step)

    remote(cots.at[c_half_in], cots.at[c_half_in], cfs.at[1], cfr.at[1], sibling).wait_recv()
    back = lax.dot_general(cots[...], lp[...], NT, preferred_element_type=F32)
    act[...] = jnp.dot(squeeze, (back * slope).astype(BF16), preferred_element_type=F32).astype(BF16)
    g = lat_chunks
    sib_out[g] = lax.dot_general(act[theirs, :], pp[...], NT, preferred_element_type=F32).astype(BF16)
    to_sibling(g).start()
    own[g] = lax.dot_general(act[mine, :], pp[...], NT, preferred_element_type=F32)
    y_step(g)

    pl.loop(0, chunks)(z_step)

    @pl.loop(0, lat_chunks)
    def _(c):
        latent_ref[:, c_cols(c)] = last_step(c)[:slots].astype(BF16)

    grad_ref[...] = jnp.where(valid, last_step(g), 0.0)[:slots].astype(BF16)

    @pl.when(chip < chips - 1)
    def _():
        @pl.loop(0, groups)
        def _(g):
            ahead(0, g).wait_send()
            ahead(1, g).wait_send()

    @pl.when((core == 0) | (chip >= 1))
    def _():
        @pl.loop(0, groups)
        def _(g):
            across(0, g).wait_send()
            across(1, g).wait_send()

    if exchange:
        p_remote.wait_send()
        l_remote.wait_send()
    for copy in cot_z + pool_z + [cot_y, cot_c, pool_y, pool_c]:
        copy.wait_send()

    @pl.loop(0, chunks)
    def _(c):
        to_sibling(c).wait_send()
        to_y(c).wait_send()
        for j in range(1, nz):
            to_z(c, j).wait_send()


def per_device(
    n,
    exchange,
    byte_queries,
    byte_keys,
    byte_values,
    patch_starts,
    patch_proj,
    latent_proj,
    latent_cotangent,
):
    rows, width = byte_queries.shape[1:]
    slots, wide = latent_cotangent.shape[1:]
    if not exchange:
        patch_proj = lax.all_gather(patch_proj, "dp", axis=0, tiled=True)
        latent_proj = lax.all_gather(latent_proj, "dp", axis=1, tiled=True)
    block = patch_proj.shape[1]
    nz = n // 4
    cw = width
    chunks = wide // cw + 1
    groups = width // 256
    half = n // 2 * slots
    vmem = pl.BlockSpec(memory_space=pltpu.VMEM)
    hbm = pl.BlockSpec(memory_space=pl.ANY)
    dma = pltpu.SemaphoreType.DMA
    latent, grads = pl.pallas_call(
        functools.partial(kernel, n, exchange),
        out_shape=(
            jax.ShapeDtypeStruct((slots, wide), BF16),
            jax.ShapeDtypeStruct((slots, width), BF16),
        ),
        in_specs=[hbm] * 7,
        out_specs=(vmem, vmem),
        scratch_shapes=[
            pltpu.SMEM((1, slots), jnp.int32),
            pltpu.VMEM((rows, width), BF16),
            pltpu.VMEM((rows, width), BF16),
            pltpu.VMEM((rows, width), BF16),
            pltpu.VMEM((slots, wide), BF16),
            pltpu.VMEM((2, rows, width), BF16),
            pltpu.VMEM((2, rows, width), BF16),
            pltpu.VMEM((rows, width), BF16),
            pltpu.VMEM((n * SLAB, width), BF16),
            pltpu.VMEM((n * SLAB, wide), BF16),
            pltpu.VMEM((width, block), BF16),
            pltpu.VMEM((block, wide), BF16),
            pltpu.VMEM((n * slots, block), BF16),
            pltpu.VMEM((chunks, half, cw), F32),
            pltpu.VMEM((chunks, half, cw), BF16),
            pltpu.VMEM((chunks, half, cw), BF16),
            pltpu.VMEM((chunks, half // 2, cw), BF16),
            pltpu.VMEM((chunks, half // 2, cw), BF16),
            pltpu.VMEM((chunks, nz * SLAB, cw), BF16),
            pltpu.VMEM((chunks, nz - 1, SLAB, cw), BF16),
            dma((5,)),
            dma((2,)),
            dma((2,)),
            dma((2,)),
            dma((2, groups)),
            dma((2, groups)),
            dma((2, groups)),
            dma((2, groups)),
            dma((nz - 1,)),
            dma((nz - 1,)),
            dma((2,)),
            dma((2,)),
            dma((nz - 1,)),
            dma((nz - 1,)),
            dma((2,)),
            dma((2,)),
            dma((chunks,)),
            dma((chunks,)),
            dma((chunks,)),
            dma((chunks,)),
            dma((chunks, nz - 1)),
            dma((chunks, nz - 1)),
        ],
        compiler_params=pltpu.CompilerParams(
            collective_id=0, has_side_effects=True, vmem_limit_bytes=60 * 2**20
        ),
        cost_estimate=pl.CostEstimate(flops=2 * 10**9, bytes_accessed=4 * 10**6, transcendentals=10**6),
    )(
        patch_starts[0],
        byte_queries[0],
        byte_keys[0],
        byte_values[0],
        latent_cotangent[0],
        patch_proj,
        latent_proj,
    )
    return latent[None], grads[None]


def solution(mesh):
    n = mesh.shape["bytes"]
    return jax.shard_map(
        functools.partial(per_device, n, mesh.shape["dp"] == 2),
        mesh=mesh,
        in_specs=(
            P("dp", "bytes", None),
            P("dp", "bytes", None),
            P("dp", "bytes", None),
            P("dp", "bytes", None),
            P("dp", "bytes"),
            P("bytes", "dp"),
            P("dp", "bytes", None),
        ),
        out_specs=(P("dp", "bytes", None), P("dp", "bytes", None)),
        check_vma=False,
    )
```

```python
import functools

import jax
import jax.numpy as jnp
from jax import lax
from jax.experimental import pallas as pl
from jax.experimental.pallas import tpu as pltpu
from jax.sharding import PartitionSpec as P

HEAD_L = 64
MESH = pl.DeviceIdType.MESH
SLAB = 16
F32 = jnp.float32
BF16 = jnp.bfloat16
NT = (((1,), (1,)), ((), ()))


def remote(src, dst, send, recv, target):
    return pltpu.make_async_remote_copy(
        src_ref=src, dst_ref=dst, send_sem=send, recv_sem=recv, device_id=target, device_id_type=MESH
    )


def kernel(
    n,
    exchange,
    starts_hbm,
    q_hbm,
    k_hbm,
    v_hbm,
    cot_hbm,
    pp_ref,
    lp_ref,
    latent_ref,
    grad_ref,
    starts_ref,
    q_ref,
    k_ref,
    v_ref,
    cot_ref,
    kbuf,
    vbuf,
    enc,
    pool,
    cots,
    pp,
    lp,
    act,
    own,
    sib_out,
    sib_in,
    y_out,
    y_in,
    z_out,
    z_in,
    in_sem,
    loc_sem,
    wsend,
    wrecv,
    ksend,
    krecv,
    ssend,
    srecv,
    pzs,
    pzr,
    pfs,
    pfr,
    czs,
    czr,
    cfs,
    cfr,
    rss,
    rsr,
    rys,
    ryr,
    rzs,
    rzr,
):
    rows, width = q_ref.shape
    d = lax.axis_index("dp")
    b = lax.axis_index("bytes")
    nz = n // 4
    chips = n // 2
    chip = b // 2
    core = b % 2
    y = chip % 2
    z = chip // 2
    groups = kbuf.shape[2] // 256
    chunks = own.shape[0]
    lat_chunks = chunks - 1
    cw = own.shape[2]
    slots = latent_ref.shape[0]
    half = n // 2 * SLAB
    quarter = half // 2
    tight = n // 2 * slots

    sibling = {"bytes": chip * 2 + 1 - core}
    y_peer = {"bytes": (z * 2 + 1 - y) * 2 + core}
    onward = {"bytes": lax.rem(chip + 1, chips) * 2 + core}
    other = jnp.where(y == 1, lax.rem(chip + 1, chips), lax.rem(chip + chips - 1, chips))

    def z_peer(j):
        return {"bytes": (lax.rem(z + j, nz) * 2 + y) * 2 + core}

    def slab(zz):
        return pl.ds(pl.multiple_of(((core * 2 + y) * nz + zz) * SLAB, SLAB), SLAB)

    y_half = pl.ds(pl.multiple_of((core * 2 + y) * quarter, SLAB), quarter)
    y_half_in = pl.ds(pl.multiple_of((core * 2 + 1 - y) * quarter, SLAB), quarter)
    c_half = pl.ds(pl.multiple_of(core * half, SLAB), half)
    c_half_in = pl.ds(pl.multiple_of((1 - core) * half, SLAB), half)

    if exchange:
        p_rows, l_cols = pp_ref.shape[0], lp_ref.shape[1]
        p_own = pl.ds(pl.multiple_of(d * p_rows, 256), p_rows)
        p_got = pl.ds(pl.multiple_of((1 - d) * p_rows, 256), p_rows)
        l_own = pl.ds(pl.multiple_of(d * l_cols, 256), l_cols)
        l_got = pl.ds(pl.multiple_of((1 - d) * l_cols, 256), l_cols)
        partner = {"dp": 1 - d}
        p_local = pltpu.make_async_copy(pp_ref, pp.at[p_own], loc_sem.at[0])
        l_local = pltpu.make_async_copy(lp_ref, lp.at[:, l_own], loc_sem.at[1])
    else:
        p_local = pltpu.make_async_copy(pp_ref, pp, loc_sem.at[0])
        l_local = pltpu.make_async_copy(lp_ref, lp, loc_sem.at[1])

    loads = [
        pltpu.make_async_copy(src, dst, in_sem.at[i])
        for i, (src, dst) in enumerate(
            (
                (cot_hbm, cot_ref),
                (starts_hbm, starts_ref),
                (q_hbm, q_ref),
                (k_hbm, k_ref),
                (v_hbm, v_ref),
            )
        )
    ]
    barrier = pltpu.get_barrier_semaphore()
    greeted = [sibling, y_peer, {"bytes": other * 2 + core}] + [z_peer(j) for j in range(1, nz)]
    if exchange:
        greeted.append(partner)
    for device in greeted:
        pl.semaphore_signal(barrier, inc=1, device_id=device, device_id_type=MESH)
    for copy in loads:
        copy.start()
    my_slab = slab(z)
    cots[my_slab, :] = jnp.zeros((SLAB, cots.shape[1]), BF16)
    loads[0].wait()
    cots[pl.ds(pl.multiple_of(((core * 2 + y) * nz + z) * SLAB, SLAB), slots), :] = cot_ref[...]
    pl.semaphore_wait(barrier, len(greeted))

    def cols(g):
        return pl.ds(pl.multiple_of(g * 256, 256), 256)

    def ahead(t, g):
        ref, buf = ((k_hbm, kbuf), (v_hbm, vbuf))[t]
        return remote(ref.at[:, cols(g)], buf.at[0, :, cols(g)], ksend.at[t, g], krecv.at[t, g], onward)

    def across(t, g):
        ref, buf = ((k_hbm, kbuf), (v_hbm, vbuf))[t]
        return remote(ref.at[:, cols(g)], buf.at[1, :, cols(g)], ssend.at[t, g], srecv.at[t, g], sibling)

    def passed(t, g):
        buf = (kbuf, vbuf)[t]
        return remote(buf.at[0, :, cols(g)], buf.at[1, :, cols(g)], ssend.at[t, g], srecv.at[t, g], sibling)

    @pl.when(chip < chips - 1)
    def _():
        @pl.loop(0, groups)
        def _(g):
            ahead(0, g).start()
            ahead(1, g).start()

    @pl.when(core == 0)
    def _():
        @pl.loop(0, groups)
        def _(g):
            across(0, g).start()
            across(1, g).start()

    if exchange:
        p_remote = remote(pp_ref, pp.at[p_own], wsend.at[0], wrecv.at[0], partner)
        l_remote = remote(lp_ref, lp.at[:, l_own], wsend.at[1], wrecv.at[1], partner)
        p_remote.start()
        l_remote.start()
    cot_z = [
        remote(cots.at[my_slab], cots.at[my_slab], czs.at[j - 1], czr.at[j - 1], z_peer(j))
        for j in range(1, nz)
    ]
    for copy in cot_z:
        copy.start()
    p_local.start()
    l_local.start()

    @pl.when(chip == 0)
    def _():
        kbuf[0] = jnp.zeros((rows, width), BF16)
        vbuf[0] = jnp.zeros((rows, width), BF16)

    @pl.when(b == 0)
    def _():
        kbuf[1] = jnp.zeros((rows, width), BF16)
        vbuf[1] = jnp.zeros((rows, width), BF16)

    loads[1].wait()
    slot_row = lax.broadcasted_iota(jnp.int32, (SLAB, rows), 0)
    place = lax.broadcasted_iota(jnp.int32, (SLAB, rows), 1)
    first = jnp.full((SLAB, rows), rows, jnp.int32)
    last = jnp.full((SLAB, rows), rows, jnp.int32)
    for p in range(slots):
        first = jnp.where(slot_row == p, starts_ref[0, p], first)
        if p + 1 < slots:
            last = jnp.where(slot_row == p, starts_ref[0, p + 1], last)
    member = jnp.where((place >= first) & (place < last), 1.0, 0.0).astype(F32)
    length = jnp.maximum(jnp.sum(member, axis=1, keepdims=True), 1.0)
    member = member.astype(BF16)
    valid = jnp.max(first, axis=1, keepdims=True) < rows

    lane = lax.broadcasted_iota(jnp.int32, (rows, 128), 1)
    query_row = lax.broadcasted_iota(jnp.int32, (2 * rows, rows), 0)
    query_row = jnp.where(query_row >= rows, query_row - rows, query_row)
    causal = lax.broadcasted_iota(jnp.int32, (2 * rows, rows), 1) <= query_row
    low = lane < HEAD_L
    far_bias = jnp.where(chip >= 1, 0.0, -1e30).astype(F32)
    mid_bias = jnp.where(b >= 1, 0.0, -1e30).astype(F32)

    def await_group(t, g):
        @pl.when(chip >= 1)
        def _():
            ahead(t, g).wait_recv()

        @pl.when((core == 1) & (chip >= 1))
        def _():
            passed(t, g).start()

        @pl.when((core == 1) | (chip >= 1))
        def _():
            across(t, g).wait_recv()

    cot_y = remote(cots.at[y_half], cots.at[y_half], cfs.at[0], cfr.at[0], y_peer)
    cot_c = remote(cots.at[c_half], cots.at[c_half], cfs.at[1], cfr.at[1], sibling)

    def await_z(buf, sends, recvs):
        for j in range(1, nz):
            from_slab = slab(lax.rem(z + nz - j, nz))
            remote(buf.at[from_slab], buf.at[from_slab], sends.at[j - 1], recvs.at[j - 1], z_peer(j)).wait_recv()

    for copy in loads[2:]:
        copy.wait()

    @pl.loop(0, groups)
    def _(g):
        await_group(0, g)
        await_group(1, g)

        @pl.when(g == groups - 1)
        def _():
            await_z(cots, czs, czr)
            cot_y.start()

        for pair in range(2):
            at = pl.ds(pl.multiple_of(g * 256 + pair * 128, 128), 128)
            q = q_ref[:, at].astype(F32) * HEAD_L ** (-0.5)
            q2 = jnp.concatenate([jnp.where(low, q, 0.0), jnp.where(low, 0.0, q)], axis=0).astype(BF16)
            s_own = lax.dot_general(q2, k_ref[:, at], NT, preferred_element_type=F32)
            s_mid = lax.dot_general(q2, kbuf[1, :, at], NT, preferred_element_type=F32) + mid_bias
            s_far = lax.dot_general(q2, kbuf[0, :, at], NT, preferred_element_type=F32) + far_bias
            s_two = jnp.where(causal, s_own, s_far)
            top = jnp.max(jnp.maximum(s_two, s_mid), axis=1, keepdims=True)
            e_two = jnp.exp(s_two - top)
            e_mid = jnp.exp(s_mid - top)
            total = jnp.sum(e_two + e_mid, axis=1, keepdims=True)
            e_own = jnp.where(causal, e_two, 0.0).astype(BF16)
            e_far = jnp.where(causal, 0.0, e_two).astype(BF16)
            mixed = jnp.dot(e_own, v_ref[:, at], preferred_element_type=F32)
            mixed += jnp.dot(e_mid.astype(BF16), vbuf[1, :, at], preferred_element_type=F32)
            mixed += jnp.dot(e_far, vbuf[0, :, at], preferred_element_type=F32)
            mixed = mixed / total
            enc[:, at] = jnp.where(low, mixed[:rows], mixed[rows:]).astype(BF16)
        summed = jnp.dot(member, enc[:, cols(g)], preferred_element_type=F32)
        pool[my_slab, cols(g)] = (summed / length).astype(BF16)

    pool_z = [
        remote(pool.at[my_slab], pool.at[my_slab], pzs.at[j - 1], pzr.at[j - 1], z_peer(j))
        for j in range(1, nz)
    ]
    for copy in pool_z:
        copy.start()
    pool_y = remote(pool.at[y_half], pool.at[y_half], pfs.at[0], pfr.at[0], y_peer)
    pool_c = remote(pool.at[c_half], pool.at[c_half], pfs.at[1], pfr.at[1], sibling)

    await_z(pool, pzs, pzr)
    pool_y.start()
    remote(pool.at[y_half_in], pool.at[y_half_in], pfs.at[0], pfr.at[0], y_peer).wait_recv()
    pool_c.start()
    remote(pool.at[c_half_in], pool.at[c_half_in], pfs.at[1], pfr.at[1], sibling).wait_recv()

    p_local.wait()
    if exchange:
        remote(pp_ref, pp.at[p_got], wsend.at[0], wrecv.at[0], partner).wait_recv()
    hidden = jnp.dot(pool[...], pp[...], preferred_element_type=F32)
    sigma = 1.0 / (1.0 + jnp.exp(-hidden))
    wide_col = lax.broadcasted_iota(jnp.int32, (n * slots, n * SLAB), 1)
    squeeze = (wide_col >> 4) * slots + (wide_col & 15) == lax.broadcasted_iota(
        jnp.int32, (n * slots, n * SLAB), 0
    )
    squeeze = jnp.where(squeeze & ((wide_col & 15) < slots), 1.0, 0.0).astype(BF16)
    wide_row = lax.broadcasted_iota(jnp.int32, (nz * SLAB, nz * slots), 0)
    spread = (wide_row >> 4) * slots + (wide_row & 15) == lax.broadcasted_iota(
        jnp.int32, (nz * SLAB, nz * slots), 1
    )
    spread = jnp.where(spread & ((wide_row & 15) < slots), 1.0, 0.0).astype(BF16)
    extra = SLAB - slots
    packs = slots // extra
    part = cw // (packs + 1)
    tight_col = lax.broadcasted_iota(jnp.int32, (nz * SLAB, nz * slots), 1)
    small_row = lax.broadcasted_iota(jnp.int32, (SLAB, SLAB), 0)
    small_col = lax.broadcasted_iota(jnp.int32, (SLAB, SLAB), 1)
    folds, unfolds = [], []
    for k in range(packs):
        fold = (wide_row >> 4) * slots + (wide_row & 15) - slots + extra * k == tight_col
        folds.append(jnp.where(fold & ((wide_row & 15) >= slots), 1.0, 0.0).astype(BF16))
        unfold = (small_col == small_row + slots - extra * k) & (small_col >= slots)
        unfolds.append(jnp.where(unfold, 1.0, 0.0).astype(BF16))
    activation = (hidden * sigma).astype(BF16)
    act[...] = jnp.dot(squeeze, activation, preferred_element_type=F32).astype(BF16)
    slope = sigma * (1.0 + hidden * (1.0 - sigma))

    l_local.wait()

    mine = pl.ds(pl.multiple_of(core * tight, SLAB), tight)
    theirs = pl.ds(pl.multiple_of((1 - core) * tight, SLAB), tight)

    def to_sibling(c):
        return remote(sib_out.at[c], sib_in.at[c], rss.at[c], rsr.at[c], sibling)

    def to_y(c):
        return remote(y_out.at[c], y_in.at[c], rys.at[c], ryr.at[c], y_peer)

    def to_z(c, j):
        there = pl.ds(pl.multiple_of(lax.rem(z + j, nz) * SLAB, SLAB), SLAB)
        return remote(z_out.at[c, there], z_in.at[c, j - 1], rzs.at[c, j - 1], rzr.at[c, j - 1], z_peer(j))

    def c_cols(c):
        if exchange:
            c = lax.rem(c + d * (lat_chunks // 2), lat_chunks)
        return pl.ds(pl.multiple_of(c * cw, 128), cw)

    def product(c):
        w = lp[:, c_cols(c)]
        sib_out[c] = jnp.dot(act[theirs, :], w, preferred_element_type=F32).astype(BF16)
        to_sibling(c).start()
        own[c] = jnp.dot(act[mine, :], w, preferred_element_type=F32)

    pl.loop(0, lat_chunks // 2)(product)
    if exchange:
        remote(lp_ref, lp.at[:, l_got], wsend.at[1], wrecv.at[1], partner).wait_recv()
    pl.loop(lat_chunks // 2, lat_chunks)(product)

    remote(cots.at[y_half_in], cots.at[y_half_in], cfs.at[0], cfr.at[0], y_peer).wait_recv()
    cot_c.start()

    def y_step(c):
        to_sibling(c).wait_recv()
        there = pl.ds(pl.multiple_of((1 - y) * (tight // 2), SLAB), tight // 2)
        here = pl.ds(pl.multiple_of(y * (tight // 2), SLAB), tight // 2)
        y_out[c] = (own[c, there, :] + sib_in[c, there, :].astype(F32)).astype(BF16)
        to_y(c).start()
        own[c, here, :] = own[c, here, :] + sib_in[c, here, :].astype(F32)

    def z_step(c):
        to_y(c).wait_recv()
        here = pl.ds(pl.multiple_of(y * (tight // 2), SLAB), tight // 2)
        total = (own[c, here, :] + y_in[c].astype(F32)).astype(BF16)
        tail = total[:, packs * part :]
        for k in range(packs):
            at = slice(k * part, (k + 1) * part)
            piece = jnp.dot(spread, total[:, at], preferred_element_type=F32)
            piece += jnp.dot(folds[k], tail, preferred_element_type=F32)
            z_out[c, :, at] = piece.astype(BF16)
        for j in range(1, nz):
            to_z(c, j).start()

    def last_step(c):
        total = z_out[c, pl.ds(pl.multiple_of(z * SLAB, SLAB), SLAB), :].astype(F32)
        for j in range(1, nz):
            to_z(c, j).wait_recv()
            total = total + z_in[c, j - 1].astype(F32)
        total = total.astype(BF16)
        tail = jnp.zeros((SLAB, part), F32)
        for k in range(packs):
            tail += jnp.dot(unfolds[k], total[:, k * part : (k + 1) * part], preferred_element_type=F32)
        return jnp.concatenate([total.astype(F32), tail], axis=1)

    pl.loop(0, lat_chunks)(y_step)

    remote(cots.at[c_half_in], cots.at[c_half_in], cfs.at[1], cfr.at[1], sibling).wait_recv()
    z_step(0)
    mid = lp.shape[1] // 2
    back = lax.dot_general(cots[:, :mid], lp[:, :mid], NT, preferred_element_type=F32)
    z_step(1)
    back += lax.dot_general(cots[:, mid:], lp[:, mid:], NT, preferred_element_type=F32)
    act[...] = jnp.dot(squeeze, (back * slope).astype(BF16), preferred_element_type=F32).astype(BF16)
    g = lat_chunks
    sib_out[g] = lax.dot_general(act[theirs, :], pp[...], NT, preferred_element_type=F32).astype(BF16)
    to_sibling(g).start()
    own[g] = lax.dot_general(act[mine, :], pp[...], NT, preferred_element_type=F32)
    z_step(2)
    y_step(g)
    pl.loop(3, chunks)(z_step)

    @pl.loop(0, lat_chunks)
    def _(c):
        latent_ref[:, c_cols(c)] = last_step(c)[:slots].astype(BF16)

    grad_ref[...] = jnp.where(valid, last_step(g), 0.0)[:slots].astype(BF16)

    @pl.when(chip < chips - 1)
    def _():
        @pl.loop(0, groups)
        def _(g):
            ahead(0, g).wait_send()
            ahead(1, g).wait_send()

    @pl.when((core == 0) | (chip >= 1))
    def _():
        @pl.loop(0, groups)
        def _(g):
            across(0, g).wait_send()
            across(1, g).wait_send()

    if exchange:
        p_remote.wait_send()
        l_remote.wait_send()
    for copy in cot_z + pool_z + [cot_y, cot_c, pool_y, pool_c]:
        copy.wait_send()

    @pl.loop(0, chunks)
    def _(c):
        to_sibling(c).wait_send()
        to_y(c).wait_send()
        for j in range(1, nz):
            to_z(c, j).wait_send()


def per_device(
    n,
    exchange,
    byte_queries,
    byte_keys,
    byte_values,
    patch_starts,
    patch_proj,
    latent_proj,
    latent_cotangent,
):
    rows, width = byte_queries.shape[1:]
    slots, wide = latent_cotangent.shape[1:]
    if not exchange:
        patch_proj = lax.all_gather(patch_proj, "dp", axis=0, tiled=True)
        latent_proj = lax.all_gather(latent_proj, "dp", axis=1, tiled=True)
    block = patch_proj.shape[1]
    nz = n // 4
    cw = width
    chunks = wide // cw + 1
    groups = width // 256
    half = n // 2 * slots
    vmem = pl.BlockSpec(memory_space=pltpu.VMEM)
    hbm = pl.BlockSpec(memory_space=pl.ANY)
    dma = pltpu.SemaphoreType.DMA
    latent, grads = pl.pallas_call(
        functools.partial(kernel, n, exchange),
        out_shape=(
            jax.ShapeDtypeStruct((slots, wide), BF16),
            jax.ShapeDtypeStruct((slots, width), BF16),
        ),
        in_specs=[hbm] * 7,
        out_specs=(vmem, vmem),
        scratch_shapes=[
            pltpu.SMEM((1, slots), jnp.int32),
            pltpu.VMEM((rows, width), BF16),
            pltpu.VMEM((rows, width), BF16),
            pltpu.VMEM((rows, width), BF16),
            pltpu.VMEM((slots, wide), BF16),
            pltpu.VMEM((2, rows, width), BF16),
            pltpu.VMEM((2, rows, width), BF16),
            pltpu.VMEM((rows, width), BF16),
            pltpu.VMEM((n * SLAB, width), BF16),
            pltpu.VMEM((n * SLAB, wide), BF16),
            pltpu.VMEM((width, block), BF16),
            pltpu.VMEM((block, wide), BF16),
            pltpu.VMEM((n * slots, block), BF16),
            pltpu.VMEM((chunks, half, cw), F32),
            pltpu.VMEM((chunks, half, cw), BF16),
            pltpu.VMEM((chunks, half, cw), BF16),
            pltpu.VMEM((chunks, half // 2, cw), BF16),
            pltpu.VMEM((chunks, half // 2, cw), BF16),
            pltpu.VMEM((chunks, nz * SLAB, cw * slots // SLAB), BF16),
            pltpu.VMEM((chunks, nz - 1, SLAB, cw * slots // SLAB), BF16),
            dma((5,)),
            dma((2,)),
            dma((2,)),
            dma((2,)),
            dma((2, groups)),
            dma((2, groups)),
            dma((2, groups)),
            dma((2, groups)),
            dma((nz - 1,)),
            dma((nz - 1,)),
            dma((2,)),
            dma((2,)),
            dma((nz - 1,)),
            dma((nz - 1,)),
            dma((2,)),
            dma((2,)),
            dma((chunks,)),
            dma((chunks,)),
            dma((chunks,)),
            dma((chunks,)),
            dma((chunks, nz - 1)),
            dma((chunks, nz - 1)),
        ],
        compiler_params=pltpu.CompilerParams(
            collective_id=0, has_side_effects=True, vmem_limit_bytes=60 * 2**20
        ),
        cost_estimate=pl.CostEstimate(flops=2 * 10**9, bytes_accessed=4 * 10**6, transcendentals=10**6),
    )(
        patch_starts[0],
        byte_queries[0],
        byte_keys[0],
        byte_values[0],
        latent_cotangent[0],
        patch_proj,
        latent_proj,
    )
    return latent[None], grads[None]


def solution(mesh):
    n = mesh.shape["bytes"]
    return jax.shard_map(
        functools.partial(per_device, n, mesh.shape["dp"] == 2),
        mesh=mesh,
        in_specs=(
            P("dp", "bytes", None),
            P("dp", "bytes", None),
            P("dp", "bytes", None),
            P("dp", "bytes", None),
            P("dp", "bytes"),
            P("bytes", "dp"),
            P("dp", "bytes", None),
        ),
        out_specs=(P("dp", "bytes", None), P("dp", "bytes", None)),
        check_vma=False,
    )
```

```python
import functools

import jax
import jax.numpy as jnp
from jax import lax
from jax.experimental import pallas as pl
from jax.experimental.pallas import tpu as pltpu
from jax.sharding import PartitionSpec as P

HEAD_L = 64
MESH = pl.DeviceIdType.MESH
SLAB = 16
F32 = jnp.float32
BF16 = jnp.bfloat16
NT = (((1,), (1,)), ((), ()))


def remote(src, dst, send, recv, target):
    return pltpu.make_async_remote_copy(
        src_ref=src, dst_ref=dst, send_sem=send, recv_sem=recv, device_id=target, device_id_type=MESH
    )


def kernel(
    n,
    exchange,
    starts_hbm,
    q_hbm,
    k_hbm,
    v_hbm,
    cot_hbm,
    pp_ref,
    lp_ref,
    latent_ref,
    grad_ref,
    starts_ref,
    q_ref,
    k_ref,
    v_ref,
    cot_ref,
    kbuf,
    vbuf,
    enc,
    pool,
    cots,
    pp,
    lp,
    act,
    own,
    sib_out,
    sib_in,
    y_out,
    y_in,
    z_out,
    z_in,
    in_sem,
    loc_sem,
    wsend,
    wrecv,
    ksend,
    krecv,
    ssend,
    srecv,
    pzs,
    pzr,
    pfs,
    pfr,
    czs,
    czr,
    cfs,
    cfr,
    rss,
    rsr,
    rys,
    ryr,
    rzs,
    rzr,
):
    rows, width = q_ref.shape
    d = lax.axis_index("dp")
    b = lax.axis_index("bytes")
    nz = n // 4
    chips = n // 2
    chip = b // 2
    core = b % 2
    y = chip % 2
    z = chip // 2
    groups = kbuf.shape[2] // 256
    chunks = own.shape[0]
    lat_chunks = chunks - 1
    cw = own.shape[2]
    slots = latent_ref.shape[0]
    half = n // 2 * SLAB
    quarter = half // 2
    tight = n // 2 * slots

    sibling = {"bytes": chip * 2 + 1 - core}
    y_peer = {"bytes": (z * 2 + 1 - y) * 2 + core}
    onward = {"bytes": lax.rem(chip + 1, chips) * 2 + core}
    other = jnp.where(y == 1, lax.rem(chip + 1, chips), lax.rem(chip + chips - 1, chips))

    def z_peer(j):
        return {"bytes": (lax.rem(z + j, nz) * 2 + y) * 2 + core}

    def slab(zz):
        return pl.ds(pl.multiple_of(((core * 2 + y) * nz + zz) * SLAB, SLAB), SLAB)

    y_half = pl.ds(pl.multiple_of((core * 2 + y) * quarter, SLAB), quarter)
    y_half_in = pl.ds(pl.multiple_of((core * 2 + 1 - y) * quarter, SLAB), quarter)
    c_half = pl.ds(pl.multiple_of(core * half, SLAB), half)
    c_half_in = pl.ds(pl.multiple_of((1 - core) * half, SLAB), half)

    if exchange:
        p_rows, l_cols = pp_ref.shape[0], lp_ref.shape[1]
        p_own = pl.ds(pl.multiple_of(d * p_rows, 256), p_rows)
        p_got = pl.ds(pl.multiple_of((1 - d) * p_rows, 256), p_rows)
        l_own = pl.ds(pl.multiple_of(d * l_cols, 256), l_cols)
        l_got = pl.ds(pl.multiple_of((1 - d) * l_cols, 256), l_cols)
        partner = {"dp": 1 - d}
        p_local = pltpu.make_async_copy(pp_ref, pp.at[p_own], loc_sem.at[0])
        l_local = pltpu.make_async_copy(lp_ref, lp.at[:, l_own], loc_sem.at[1])
    else:
        p_local = pltpu.make_async_copy(pp_ref, pp, loc_sem.at[0])
        l_local = pltpu.make_async_copy(lp_ref, lp, loc_sem.at[1])

    loads = [
        pltpu.make_async_copy(src, dst, in_sem.at[i])
        for i, (src, dst) in enumerate(
            (
                (cot_hbm, cot_ref),
                (starts_hbm, starts_ref),
                (q_hbm, q_ref),
                (k_hbm, k_ref),
                (v_hbm, v_ref),
            )
        )
    ]
    barrier = pltpu.get_barrier_semaphore()
    greeted = [sibling, y_peer, {"bytes": other * 2 + core}] + [z_peer(j) for j in range(1, nz)]
    if exchange:
        greeted.append(partner)
    for device in greeted:
        pl.semaphore_signal(barrier, inc=1, device_id=device, device_id_type=MESH)
    for copy in loads:
        copy.start()
    my_slab = slab(z)
    cots[my_slab, :] = jnp.zeros((SLAB, cots.shape[1]), BF16)
    loads[0].wait()
    cots[pl.ds(pl.multiple_of(((core * 2 + y) * nz + z) * SLAB, SLAB), slots), :] = cot_ref[...]
    pl.semaphore_wait(barrier, len(greeted))

    def cols(g):
        return pl.ds(pl.multiple_of(g * 256, 256), 256)

    def ahead(t, g):
        ref, buf = ((k_hbm, kbuf), (v_hbm, vbuf))[t]
        return remote(ref.at[:, cols(g)], buf.at[0, :, cols(g)], ksend.at[t, g], krecv.at[t, g], onward)

    def across(t, g):
        ref, buf = ((k_hbm, kbuf), (v_hbm, vbuf))[t]
        return remote(ref.at[:, cols(g)], buf.at[1, :, cols(g)], ssend.at[t, g], srecv.at[t, g], sibling)

    def passed(t, g):
        buf = (kbuf, vbuf)[t]
        return remote(buf.at[0, :, cols(g)], buf.at[1, :, cols(g)], ssend.at[t, g], srecv.at[t, g], sibling)

    @pl.when(chip < chips - 1)
    def _():
        @pl.loop(0, groups)
        def _(g):
            ahead(0, g).start()
            ahead(1, g).start()

    @pl.when(core == 0)
    def _():
        @pl.loop(0, groups)
        def _(g):
            across(0, g).start()
            across(1, g).start()

    if exchange:
        p_remote = remote(pp_ref, pp.at[p_own], wsend.at[0], wrecv.at[0], partner)
        l_remote = remote(lp_ref, lp.at[:, l_own], wsend.at[1], wrecv.at[1], partner)
        p_remote.start()
        l_remote.start()
    cot_z = [
        remote(cots.at[my_slab], cots.at[my_slab], czs.at[j - 1], czr.at[j - 1], z_peer(j))
        for j in range(1, nz)
    ]
    p_local.start()
    l_local.start()

    @pl.when(chip == 0)
    def _():
        kbuf[0] = jnp.zeros((rows, width), BF16)
        vbuf[0] = jnp.zeros((rows, width), BF16)

    @pl.when(b == 0)
    def _():
        kbuf[1] = jnp.zeros((rows, width), BF16)
        vbuf[1] = jnp.zeros((rows, width), BF16)

    loads[1].wait()
    slot_row = lax.broadcasted_iota(jnp.int32, (SLAB, rows), 0)
    place = lax.broadcasted_iota(jnp.int32, (SLAB, rows), 1)
    first = jnp.full((SLAB, rows), rows, jnp.int32)
    last = jnp.full((SLAB, rows), rows, jnp.int32)
    for p in range(slots):
        first = jnp.where(slot_row == p, starts_ref[0, p], first)
        if p + 1 < slots:
            last = jnp.where(slot_row == p, starts_ref[0, p + 1], last)
    member = jnp.where((place >= first) & (place < last), 1.0, 0.0).astype(F32)
    length = jnp.maximum(jnp.sum(member, axis=1, keepdims=True), 1.0)
    member = member.astype(BF16)
    valid = jnp.max(first, axis=1, keepdims=True) < rows

    lane = lax.broadcasted_iota(jnp.int32, (rows, 128), 1)
    query_row = lax.broadcasted_iota(jnp.int32, (2 * rows, rows), 0)
    query_row = jnp.where(query_row >= rows, query_row - rows, query_row)
    causal = lax.broadcasted_iota(jnp.int32, (2 * rows, rows), 1) <= query_row
    low = lane < HEAD_L
    far_bias = jnp.where(chip >= 1, 0.0, -1e30).astype(F32)
    mid_bias = jnp.where(b >= 1, 0.0, -1e30).astype(F32)

    def await_group(t, g):
        @pl.when(chip >= 1)
        def _():
            ahead(t, g).wait_recv()

        @pl.when((core == 1) & (chip >= 1))
        def _():
            passed(t, g).start()

        @pl.when((core == 1) | (chip >= 1))
        def _():
            across(t, g).wait_recv()

    cot_y = remote(cots.at[y_half], cots.at[y_half], cfs.at[0], cfr.at[0], y_peer)
    cot_c = remote(cots.at[c_half], cots.at[c_half], cfs.at[1], cfr.at[1], sibling)

    def await_z(buf, sends, recvs):
        for j in range(1, nz):
            from_slab = slab(lax.rem(z + nz - j, nz))
            remote(buf.at[from_slab], buf.at[from_slab], sends.at[j - 1], recvs.at[j - 1], z_peer(j)).wait_recv()

    for copy in loads[2:]:
        copy.wait()

    @pl.loop(0, groups)
    def _(g):
        await_group(0, g)
        await_group(1, g)

        @pl.when(g == groups - 1)
        def _():
            for copy in cot_z:
                copy.start()

        for pair in range(2):
            at = pl.ds(pl.multiple_of(g * 256 + pair * 128, 128), 128)
            q = q_ref[:, at].astype(F32) * HEAD_L ** (-0.5)
            q2 = jnp.concatenate([jnp.where(low, q, 0.0), jnp.where(low, 0.0, q)], axis=0).astype(BF16)
            s_own = lax.dot_general(q2, k_ref[:, at], NT, preferred_element_type=F32)
            s_mid = lax.dot_general(q2, kbuf[1, :, at], NT, preferred_element_type=F32) + mid_bias
            s_far = lax.dot_general(q2, kbuf[0, :, at], NT, preferred_element_type=F32) + far_bias
            s_two = jnp.where(causal, s_own, s_far)
            top = jnp.max(jnp.maximum(s_two, s_mid), axis=1, keepdims=True)
            e_two = jnp.exp(s_two - top)
            e_mid = jnp.exp(s_mid - top)
            total = jnp.sum(e_two + e_mid, axis=1, keepdims=True)
            e_own = jnp.where(causal, e_two, 0.0).astype(BF16)
            e_far = jnp.where(causal, 0.0, e_two).astype(BF16)
            mixed = jnp.dot(e_own, v_ref[:, at], preferred_element_type=F32)
            mixed += jnp.dot(e_mid.astype(BF16), vbuf[1, :, at], preferred_element_type=F32)
            mixed += jnp.dot(e_far, vbuf[0, :, at], preferred_element_type=F32)
            mixed = mixed / total
            enc[:, at] = jnp.where(low, mixed[:rows], mixed[rows:]).astype(BF16)
        summed = jnp.dot(member, enc[:, cols(g)], preferred_element_type=F32)
        pool[my_slab, cols(g)] = (summed / length).astype(BF16)

    pool_z = [
        remote(pool.at[my_slab], pool.at[my_slab], pzs.at[j - 1], pzr.at[j - 1], z_peer(j))
        for j in range(1, nz)
    ]
    for copy in pool_z:
        copy.start()
    pool_y = remote(pool.at[y_half], pool.at[y_half], pfs.at[0], pfr.at[0], y_peer)
    pool_c = remote(pool.at[c_half], pool.at[c_half], pfs.at[1], pfr.at[1], sibling)

    await_z(pool, pzs, pzr)
    pool_y.start()
    remote(pool.at[y_half_in], pool.at[y_half_in], pfs.at[0], pfr.at[0], y_peer).wait_recv()
    pool_c.start()
    await_z(cots, czs, czr)
    cot_y.start()
    remote(pool.at[c_half_in], pool.at[c_half_in], pfs.at[1], pfr.at[1], sibling).wait_recv()

    p_local.wait()
    if exchange:
        remote(pp_ref, pp.at[p_got], wsend.at[0], wrecv.at[0], partner).wait_recv()
    hidden = jnp.dot(pool[...], pp[...], preferred_element_type=F32)
    sigma = 1.0 / (1.0 + jnp.exp(-hidden))
    wide_col = lax.broadcasted_iota(jnp.int32, (n * slots, n * SLAB), 1)
    squeeze = (wide_col >> 4) * slots + (wide_col & 15) == lax.broadcasted_iota(
        jnp.int32, (n * slots, n * SLAB), 0
    )
    squeeze = jnp.where(squeeze & ((wide_col & 15) < slots), 1.0, 0.0).astype(BF16)
    wide_row = lax.broadcasted_iota(jnp.int32, (nz * SLAB, nz * slots), 0)
    spread = (wide_row >> 4) * slots + (wide_row & 15) == lax.broadcasted_iota(
        jnp.int32, (nz * SLAB, nz * slots), 1
    )
    spread = jnp.where(spread & ((wide_row & 15) < slots), 1.0, 0.0).astype(BF16)
    extra = SLAB - slots
    packs = slots // extra
    part = cw // (packs + 1)
    tight_col = lax.broadcasted_iota(jnp.int32, (nz * SLAB, nz * slots), 1)
    small_row = lax.broadcasted_iota(jnp.int32, (SLAB, SLAB), 0)
    small_col = lax.broadcasted_iota(jnp.int32, (SLAB, SLAB), 1)
    folds, unfolds = [], []
    for k in range(packs):
        fold = (wide_row >> 4) * slots + (wide_row & 15) - slots + extra * k == tight_col
        folds.append(jnp.where(fold & ((wide_row & 15) >= slots), 1.0, 0.0).astype(BF16))
        unfold = (small_col == small_row + slots - extra * k) & (small_col >= slots)
        unfolds.append(jnp.where(unfold, 1.0, 0.0).astype(BF16))
    activation = (hidden * sigma).astype(BF16)
    act[...] = jnp.dot(squeeze, activation, preferred_element_type=F32).astype(BF16)
    slope = sigma * (1.0 + hidden * (1.0 - sigma))

    l_local.wait()

    mine = pl.ds(pl.multiple_of(core * tight, SLAB), tight)
    theirs = pl.ds(pl.multiple_of((1 - core) * tight, SLAB), tight)

    def to_sibling(c):
        return remote(sib_out.at[c], sib_in.at[c], rss.at[c], rsr.at[c], sibling)

    def to_y(c):
        return remote(y_out.at[c], y_in.at[c], rys.at[c], ryr.at[c], y_peer)

    def to_z(c, j):
        there = pl.ds(pl.multiple_of(lax.rem(z + j, nz) * SLAB, SLAB), SLAB)
        return remote(z_out.at[c, there], z_in.at[c, j - 1], rzs.at[c, j - 1], rzr.at[c, j - 1], z_peer(j))

    def c_cols(c):
        if exchange:
            c = lax.rem(c + d * (lat_chunks // 2), lat_chunks)
        return pl.ds(pl.multiple_of(c * cw, 128), cw)

    def product(c):
        w = lp[:, c_cols(c)]
        sib_out[c] = jnp.dot(act[theirs, :], w, preferred_element_type=F32).astype(BF16)
        to_sibling(c).start()
        own[c] = jnp.dot(act[mine, :], w, preferred_element_type=F32)

    pl.loop(0, lat_chunks // 2)(product)
    if exchange:
        remote(lp_ref, lp.at[:, l_got], wsend.at[1], wrecv.at[1], partner).wait_recv()
    pl.loop(lat_chunks // 2, lat_chunks)(product)

    def y_step(c):
        to_sibling(c).wait_recv()
        there = pl.ds(pl.multiple_of((1 - y) * (tight // 2), SLAB), tight // 2)
        here = pl.ds(pl.multiple_of(y * (tight // 2), SLAB), tight // 2)
        y_out[c] = (own[c, there, :] + sib_in[c, there, :].astype(F32)).astype(BF16)
        to_y(c).start()
        own[c, here, :] = own[c, here, :] + sib_in[c, here, :].astype(F32)

    def z_step(c):
        to_y(c).wait_recv()
        here = pl.ds(pl.multiple_of(y * (tight // 2), SLAB), tight // 2)
        total = (own[c, here, :] + y_in[c].astype(F32)).astype(BF16)
        tail = total[:, packs * part :]
        for k in range(packs):
            at = slice(k * part, (k + 1) * part)
            piece = jnp.dot(spread, total[:, at], preferred_element_type=F32)
            piece += jnp.dot(folds[k], tail, preferred_element_type=F32)
            z_out[c, :, at] = piece.astype(BF16)
        for j in range(1, nz):
            to_z(c, j).start()

    def last_step(c):
        total = z_out[c, pl.ds(pl.multiple_of(z * SLAB, SLAB), SLAB), :].astype(F32)
        for j in range(1, nz):
            to_z(c, j).wait_recv()
            total = total + z_in[c, j - 1].astype(F32)
        total = total.astype(BF16)
        tail = jnp.zeros((SLAB, part), F32)
        for k in range(packs):
            tail += jnp.dot(unfolds[k], total[:, k * part : (k + 1) * part], preferred_element_type=F32)
        return jnp.concatenate([total.astype(F32), tail], axis=1)

    pl.loop(0, lat_chunks)(y_step)

    pl.loop(0, 2)(z_step)
    remote(cots.at[y_half_in], cots.at[y_half_in], cfs.at[0], cfr.at[0], y_peer).wait_recv()
    cot_c.start()
    pl.loop(2, lat_chunks)(z_step)
    remote(cots.at[c_half_in], cots.at[c_half_in], cfs.at[1], cfr.at[1], sibling).wait_recv()
    back = lax.dot_general(cots[...], lp[...], NT, preferred_element_type=F32)
    act[...] = jnp.dot(squeeze, (back * slope).astype(BF16), preferred_element_type=F32).astype(BF16)
    g = lat_chunks
    sib_out[g] = lax.dot_general(act[theirs, :], pp[...], NT, preferred_element_type=F32).astype(BF16)
    to_sibling(g).start()
    own[g] = lax.dot_general(act[mine, :], pp[...], NT, preferred_element_type=F32)
    y_step(g)
    z_step(g)

    @pl.loop(0, lat_chunks)
    def _(c):
        latent_ref[:, c_cols(c)] = last_step(c)[:slots].astype(BF16)

    grad_ref[...] = jnp.where(valid, last_step(g), 0.0)[:slots].astype(BF16)

    @pl.when(chip < chips - 1)
    def _():
        @pl.loop(0, groups)
        def _(g):
            ahead(0, g).wait_send()
            ahead(1, g).wait_send()

    @pl.when((core == 0) | (chip >= 1))
    def _():
        @pl.loop(0, groups)
        def _(g):
            across(0, g).wait_send()
            across(1, g).wait_send()

    if exchange:
        p_remote.wait_send()
        l_remote.wait_send()
    for copy in cot_z + pool_z + [cot_y, cot_c, pool_y, pool_c]:
        copy.wait_send()

    @pl.loop(0, chunks)
    def _(c):
        to_sibling(c).wait_send()
        to_y(c).wait_send()
        for j in range(1, nz):
            to_z(c, j).wait_send()


def per_device(
    n,
    exchange,
    byte_queries,
    byte_keys,
    byte_values,
    patch_starts,
    patch_proj,
    latent_proj,
    latent_cotangent,
):
    rows, width = byte_queries.shape[1:]
    slots, wide = latent_cotangent.shape[1:]
    if not exchange:
        patch_proj = lax.all_gather(patch_proj, "dp", axis=0, tiled=True)
        latent_proj = lax.all_gather(latent_proj, "dp", axis=1, tiled=True)
    block = patch_proj.shape[1]
    nz = n // 4
    cw = width
    chunks = wide // cw + 1
    groups = width // 256
    half = n // 2 * slots
    vmem = pl.BlockSpec(memory_space=pltpu.VMEM)
    hbm = pl.BlockSpec(memory_space=pl.ANY)
    dma = pltpu.SemaphoreType.DMA
    latent, grads = pl.pallas_call(
        functools.partial(kernel, n, exchange),
        out_shape=(
            jax.ShapeDtypeStruct((slots, wide), BF16),
            jax.ShapeDtypeStruct((slots, width), BF16),
        ),
        in_specs=[hbm] * 7,
        out_specs=(vmem, vmem),
        scratch_shapes=[
            pltpu.SMEM((1, slots), jnp.int32),
            pltpu.VMEM((rows, width), BF16),
            pltpu.VMEM((rows, width), BF16),
            pltpu.VMEM((rows, width), BF16),
            pltpu.VMEM((slots, wide), BF16),
            pltpu.VMEM((2, rows, width), BF16),
            pltpu.VMEM((2, rows, width), BF16),
            pltpu.VMEM((rows, width), BF16),
            pltpu.VMEM((n * SLAB, width), BF16),
            pltpu.VMEM((n * SLAB, wide), BF16),
            pltpu.VMEM((width, block), BF16),
            pltpu.VMEM((block, wide), BF16),
            pltpu.VMEM((n * slots, block), BF16),
            pltpu.VMEM((chunks, half, cw), F32),
            pltpu.VMEM((chunks, half, cw), BF16),
            pltpu.VMEM((chunks, half, cw), BF16),
            pltpu.VMEM((chunks, half // 2, cw), BF16),
            pltpu.VMEM((chunks, half // 2, cw), BF16),
            pltpu.VMEM((chunks, nz * SLAB, cw * slots // SLAB), BF16),
            pltpu.VMEM((chunks, nz - 1, SLAB, cw * slots // SLAB), BF16),
            dma((5,)),
            dma((2,)),
            dma((2,)),
            dma((2,)),
            dma((2, groups)),
            dma((2, groups)),
            dma((2, groups)),
            dma((2, groups)),
            dma((nz - 1,)),
            dma((nz - 1,)),
            dma((2,)),
            dma((2,)),
            dma((nz - 1,)),
            dma((nz - 1,)),
            dma((2,)),
            dma((2,)),
            dma((chunks,)),
            dma((chunks,)),
            dma((chunks,)),
            dma((chunks,)),
            dma((chunks, nz - 1)),
            dma((chunks, nz - 1)),
        ],
        compiler_params=pltpu.CompilerParams(
            collective_id=0, has_side_effects=True, vmem_limit_bytes=60 * 2**20
        ),
        cost_estimate=pl.CostEstimate(flops=2 * 10**9, bytes_accessed=4 * 10**6, transcendentals=10**6),
    )(
        patch_starts[0],
        byte_queries[0],
        byte_keys[0],
        byte_values[0],
        latent_cotangent[0],
        patch_proj,
        latent_proj,
    )
    return latent[None], grads[None]


def solution(mesh):
    n = mesh.shape["bytes"]
    return jax.shard_map(
        functools.partial(per_device, n, mesh.shape["dp"] == 2),
        mesh=mesh,
        in_specs=(
            P("dp", "bytes", None),
            P("dp", "bytes", None),
            P("dp", "bytes", None),
            P("dp", "bytes", None),
            P("dp", "bytes"),
            P("bytes", "dp"),
            P("dp", "bytes", None),
        ),
        out_specs=(P("dp", "bytes", None), P("dp", "bytes", None)),
        check_vma=False,
    )
```

```python
import functools

import jax
import jax.numpy as jnp
from jax import lax
from jax.experimental import pallas as pl
from jax.experimental.pallas import tpu as pltpu
from jax.sharding import PartitionSpec as P

HEAD_L = 64
MESH = pl.DeviceIdType.MESH
SLAB = 16
F32 = jnp.float32
BF16 = jnp.bfloat16
NT = (((1,), (1,)), ((), ()))


def remote(src, dst, send, recv, target):
    return pltpu.make_async_remote_copy(
        src_ref=src, dst_ref=dst, send_sem=send, recv_sem=recv, device_id=target, device_id_type=MESH
    )


def kernel(
    n,
    exchange,
    starts_hbm,
    q_hbm,
    k_hbm,
    v_hbm,
    cot_hbm,
    pp_ref,
    lp_ref,
    latent_ref,
    grad_ref,
    starts_ref,
    q_ref,
    k_ref,
    v_ref,
    cot_ref,
    kbuf,
    vbuf,
    enc,
    pool,
    cots,
    pp,
    lp,
    act,
    own,
    sib_out,
    sib_in,
    y_out,
    y_in,
    z_out,
    z_in,
    in_sem,
    loc_sem,
    wsend,
    wrecv,
    ksend,
    krecv,
    ssend,
    srecv,
    pzs,
    pzr,
    pfs,
    pfr,
    czs,
    czr,
    cfs,
    cfr,
    rss,
    rsr,
    rys,
    ryr,
    rzs,
    rzr,
):
    rows, width = q_ref.shape
    d = lax.axis_index("dp")
    b = lax.axis_index("bytes")
    nz = n // 4
    chips = n // 2
    chip = b // 2
    core = b % 2
    y = chip % 2
    z = chip // 2
    groups = kbuf.shape[2] // 256
    chunks = own.shape[0]
    lat_chunks = chunks - 1
    cw = own.shape[2]
    slots = latent_ref.shape[0]
    half = n // 2 * SLAB
    quarter = half // 2
    tight = n // 2 * slots

    sibling = {"bytes": chip * 2 + 1 - core}
    y_peer = {"bytes": (z * 2 + 1 - y) * 2 + core}
    onward = {"bytes": lax.rem(chip + 1, chips) * 2 + core}
    other = jnp.where(y == 1, lax.rem(chip + 1, chips), lax.rem(chip + chips - 1, chips))

    def z_peer(j):
        return {"bytes": (lax.rem(z + j, nz) * 2 + y) * 2 + core}

    def slab(zz):
        return pl.ds(pl.multiple_of(((core * 2 + y) * nz + zz) * SLAB, SLAB), SLAB)

    y_half = pl.ds(pl.multiple_of((core * 2 + y) * quarter, SLAB), quarter)
    y_half_in = pl.ds(pl.multiple_of((core * 2 + 1 - y) * quarter, SLAB), quarter)
    c_half = pl.ds(pl.multiple_of(core * half, SLAB), half)
    c_half_in = pl.ds(pl.multiple_of((1 - core) * half, SLAB), half)

    if exchange:
        p_rows, l_cols = pp_ref.shape[0], lp_ref.shape[1]
        p_own = pl.ds(pl.multiple_of(d * p_rows, 256), p_rows)
        p_got = pl.ds(pl.multiple_of((1 - d) * p_rows, 256), p_rows)
        l_own = pl.ds(pl.multiple_of(d * l_cols, 256), l_cols)
        l_got = pl.ds(pl.multiple_of((1 - d) * l_cols, 256), l_cols)
        partner = {"dp": 1 - d}
        p_local = pltpu.make_async_copy(pp_ref, pp.at[p_own], loc_sem.at[0])
        l_local = pltpu.make_async_copy(lp_ref, lp.at[:, l_own], loc_sem.at[1])
    else:
        p_local = pltpu.make_async_copy(pp_ref, pp, loc_sem.at[0])
        l_local = pltpu.make_async_copy(lp_ref, lp, loc_sem.at[1])

    loads = [
        pltpu.make_async_copy(src, dst, in_sem.at[i])
        for i, (src, dst) in enumerate(
            (
                (cot_hbm, cot_ref),
                (starts_hbm, starts_ref),
                (q_hbm, q_ref),
                (k_hbm, k_ref),
                (v_hbm, v_ref),
            )
        )
    ]
    barrier = pltpu.get_barrier_semaphore()
    greeted = [sibling, y_peer, {"bytes": other * 2 + core}] + [z_peer(j) for j in range(1, nz)]
    if exchange:
        greeted.append(partner)
    for device in greeted:
        pl.semaphore_signal(barrier, inc=1, device_id=device, device_id_type=MESH)
    for copy in loads:
        copy.start()
    my_slab = slab(z)
    cots[my_slab, :] = jnp.zeros((SLAB, cots.shape[1]), BF16)
    loads[0].wait()
    cots[pl.ds(pl.multiple_of(((core * 2 + y) * nz + z) * SLAB, SLAB), slots), :] = cot_ref[...]
    pl.semaphore_wait(barrier, len(greeted))

    def cols(g):
        return pl.ds(pl.multiple_of(g * 256, 256), 256)

    def ahead(t, g):
        ref, buf = ((k_hbm, kbuf), (v_hbm, vbuf))[t]
        return remote(ref.at[:, cols(g)], buf.at[0, :, cols(g)], ksend.at[t, g], krecv.at[t, g], onward)

    def across(t, g):
        ref, buf = ((k_hbm, kbuf), (v_hbm, vbuf))[t]
        return remote(ref.at[:, cols(g)], buf.at[1, :, cols(g)], ssend.at[t, g], srecv.at[t, g], sibling)

    def passed(t, g):
        buf = (kbuf, vbuf)[t]
        return remote(buf.at[0, :, cols(g)], buf.at[1, :, cols(g)], ssend.at[t, g], srecv.at[t, g], sibling)

    @pl.when(chip < chips - 1)
    def _():
        @pl.loop(0, groups)
        def _(g):
            ahead(0, g).start()
            ahead(1, g).start()

    @pl.when(core == 0)
    def _():
        @pl.loop(0, groups)
        def _(g):
            across(0, g).start()
            across(1, g).start()

    if exchange:
        p_remote = remote(pp_ref, pp.at[p_own], wsend.at[0], wrecv.at[0], partner)
        l_remote = remote(lp_ref, lp.at[:, l_own], wsend.at[1], wrecv.at[1], partner)
        p_remote.start()
        l_remote.start()
    cot_z = [
        remote(cots.at[my_slab], cots.at[my_slab], czs.at[j - 1], czr.at[j - 1], z_peer(j))
        for j in range(1, nz)
    ]
    p_local.start()
    l_local.start()

    @pl.when(chip == 0)
    def _():
        kbuf[0] = jnp.zeros((rows, width), BF16)
        vbuf[0] = jnp.zeros((rows, width), BF16)

    @pl.when(b == 0)
    def _():
        kbuf[1] = jnp.zeros((rows, width), BF16)
        vbuf[1] = jnp.zeros((rows, width), BF16)

    loads[1].wait()
    slot_row = lax.broadcasted_iota(jnp.int32, (SLAB, rows), 0)
    place = lax.broadcasted_iota(jnp.int32, (SLAB, rows), 1)
    first = jnp.full((SLAB, rows), rows, jnp.int32)
    last = jnp.full((SLAB, rows), rows, jnp.int32)
    for p in range(slots):
        first = jnp.where(slot_row == p, starts_ref[0, p], first)
        if p + 1 < slots:
            last = jnp.where(slot_row == p, starts_ref[0, p + 1], last)
    member = jnp.where((place >= first) & (place < last), 1.0, 0.0).astype(F32)
    length = jnp.maximum(jnp.sum(member, axis=1, keepdims=True), 1.0)
    member = member.astype(BF16)
    valid = jnp.max(first, axis=1, keepdims=True) < rows

    lane = lax.broadcasted_iota(jnp.int32, (rows, 128), 1)
    query_row = lax.broadcasted_iota(jnp.int32, (2 * rows, rows), 0)
    query_row = jnp.where(query_row >= rows, query_row - rows, query_row)
    causal = lax.broadcasted_iota(jnp.int32, (2 * rows, rows), 1) <= query_row
    low = lane < HEAD_L
    far_bias = jnp.where(chip >= 1, 0.0, -1e30).astype(F32)
    mid_bias = jnp.where(b >= 1, 0.0, -1e30).astype(F32)

    def await_group(t, g):
        @pl.when(chip >= 1)
        def _():
            ahead(t, g).wait_recv()

        @pl.when((core == 1) & (chip >= 1))
        def _():
            passed(t, g).start()

        @pl.when((core == 1) | (chip >= 1))
        def _():
            across(t, g).wait_recv()

    cot_y = remote(cots.at[y_half], cots.at[y_half], cfs.at[0], cfr.at[0], y_peer)
    cot_c = remote(cots.at[c_half], cots.at[c_half], cfs.at[1], cfr.at[1], sibling)

    def await_z(buf, sends, recvs):
        for j in range(1, nz):
            from_slab = slab(lax.rem(z + nz - j, nz))
            remote(buf.at[from_slab], buf.at[from_slab], sends.at[j - 1], recvs.at[j - 1], z_peer(j)).wait_recv()

    for copy in loads[2:]:
        copy.wait()

    @pl.loop(0, groups)
    def _(g):
        await_group(0, g)
        await_group(1, g)

        @pl.when(g == groups - 1)
        def _():
            for copy in cot_z:
                copy.start()

        for pair in range(2):
            at = pl.ds(pl.multiple_of(g * 256 + pair * 128, 128), 128)
            q = q_ref[:, at].astype(F32) * HEAD_L ** (-0.5)
            q2 = jnp.concatenate([jnp.where(low, q, 0.0), jnp.where(low, 0.0, q)], axis=0).astype(BF16)
            s_own = lax.dot_general(q2, k_ref[:, at], NT, preferred_element_type=F32)
            s_mid = lax.dot_general(q2, kbuf[1, :, at], NT, preferred_element_type=F32) + mid_bias
            s_far = lax.dot_general(q2, kbuf[0, :, at], NT, preferred_element_type=F32) + far_bias
            s_two = jnp.where(causal, s_own, s_far)
            top = jnp.max(jnp.maximum(s_two, s_mid), axis=1, keepdims=True)
            e_two = jnp.exp(s_two - top)
            e_mid = jnp.exp(s_mid - top)
            total = jnp.sum(e_two + e_mid, axis=1, keepdims=True)
            e_own = jnp.where(causal, e_two, 0.0).astype(BF16)
            e_far = jnp.where(causal, 0.0, e_two).astype(BF16)
            mixed = jnp.dot(e_own, v_ref[:, at], preferred_element_type=F32)
            mixed += jnp.dot(e_mid.astype(BF16), vbuf[1, :, at], preferred_element_type=F32)
            mixed += jnp.dot(e_far, vbuf[0, :, at], preferred_element_type=F32)
            mixed = mixed / total
            enc[:, at] = jnp.where(low, mixed[:rows], mixed[rows:]).astype(BF16)
        summed = jnp.dot(member, enc[:, cols(g)], preferred_element_type=F32)
        pool[my_slab, cols(g)] = (summed / length).astype(BF16)

    pool_z = [
        remote(pool.at[my_slab], pool.at[my_slab], pzs.at[j - 1], pzr.at[j - 1], z_peer(j))
        for j in range(1, nz)
    ]
    for copy in pool_z:
        copy.start()
    pool_y = remote(pool.at[y_half], pool.at[y_half], pfs.at[0], pfr.at[0], y_peer)
    pool_c = remote(pool.at[c_half], pool.at[c_half], pfs.at[1], pfr.at[1], sibling)

    await_z(pool, pzs, pzr)
    pool_y.start()
    remote(pool.at[y_half_in], pool.at[y_half_in], pfs.at[0], pfr.at[0], y_peer).wait_recv()
    pool_c.start()
    remote(pool.at[c_half_in], pool.at[c_half_in], pfs.at[1], pfr.at[1], sibling).wait_recv()

    p_local.wait()
    if exchange:
        remote(pp_ref, pp.at[p_got], wsend.at[0], wrecv.at[0], partner).wait_recv()
    hidden = jnp.dot(pool[...], pp[...], preferred_element_type=F32)
    sigma = 1.0 / (1.0 + jnp.exp(-hidden))
    wide_col = lax.broadcasted_iota(jnp.int32, (n * slots, n * SLAB), 1)
    squeeze = (wide_col >> 4) * slots + (wide_col & 15) == lax.broadcasted_iota(
        jnp.int32, (n * slots, n * SLAB), 0
    )
    squeeze = jnp.where(squeeze & ((wide_col & 15) < slots), 1.0, 0.0).astype(BF16)
    wide_row = lax.broadcasted_iota(jnp.int32, (nz * SLAB, nz * slots), 0)
    spread = (wide_row >> 4) * slots + (wide_row & 15) == lax.broadcasted_iota(
        jnp.int32, (nz * SLAB, nz * slots), 1
    )
    spread = jnp.where(spread & ((wide_row & 15) < slots), 1.0, 0.0).astype(BF16)
    extra = SLAB - slots
    packs = slots // extra
    part = cw // (packs + 1)
    tight_col = lax.broadcasted_iota(jnp.int32, (nz * SLAB, nz * slots), 1)
    small_row = lax.broadcasted_iota(jnp.int32, (SLAB, SLAB), 0)
    small_col = lax.broadcasted_iota(jnp.int32, (SLAB, SLAB), 1)
    folds, unfolds = [], []
    for k in range(packs):
        fold = (wide_row >> 4) * slots + (wide_row & 15) - slots + extra * k == tight_col
        folds.append(jnp.where(fold & ((wide_row & 15) >= slots), 1.0, 0.0).astype(BF16))
        unfold = (small_col == small_row + slots - extra * k) & (small_col >= slots)
        unfolds.append(jnp.where(unfold, 1.0, 0.0).astype(BF16))
    activation = (hidden * sigma).astype(BF16)
    act[...] = jnp.dot(squeeze, activation, preferred_element_type=F32).astype(BF16)
    slope = sigma * (1.0 + hidden * (1.0 - sigma))

    l_local.wait()

    mine = pl.ds(pl.multiple_of(core * tight, SLAB), tight)
    theirs = pl.ds(pl.multiple_of((1 - core) * tight, SLAB), tight)

    def to_sibling(c):
        return remote(sib_out.at[c], sib_in.at[c], rss.at[c], rsr.at[c], sibling)

    def to_y(c):
        return remote(y_out.at[c], y_in.at[c], rys.at[c], ryr.at[c], y_peer)

    def to_z(c, j):
        there = pl.ds(pl.multiple_of(lax.rem(z + j, nz) * SLAB, SLAB), SLAB)
        return remote(z_out.at[c, there], z_in.at[c, j - 1], rzs.at[c, j - 1], rzr.at[c, j - 1], z_peer(j))

    def c_cols(c):
        if exchange:
            c = lax.rem(c + d * (lat_chunks // 2), lat_chunks)
        return pl.ds(pl.multiple_of(c * cw, 128), cw)

    def product(c):
        w = lp[:, c_cols(c)]
        sib_out[c] = jnp.dot(act[theirs, :], w, preferred_element_type=F32).astype(BF16)
        to_sibling(c).start()
        own[c] = jnp.dot(act[mine, :], w, preferred_element_type=F32)

    pl.loop(0, lat_chunks // 2)(product)
    await_z(cots, czs, czr)
    cot_y.start()
    if exchange:
        remote(lp_ref, lp.at[:, l_got], wsend.at[1], wrecv.at[1], partner).wait_recv()
    pl.loop(lat_chunks // 2, lat_chunks)(product)

    def y_step(c):
        to_sibling(c).wait_recv()
        there = pl.ds(pl.multiple_of((1 - y) * (tight // 2), SLAB), tight // 2)
        here = pl.ds(pl.multiple_of(y * (tight // 2), SLAB), tight // 2)
        y_out[c] = (own[c, there, :] + sib_in[c, there, :].astype(F32)).astype(BF16)
        to_y(c).start()
        own[c, here, :] = own[c, here, :] + sib_in[c, here, :].astype(F32)

    def z_step(c):
        to_y(c).wait_recv()
        here = pl.ds(pl.multiple_of(y * (tight // 2), SLAB), tight // 2)
        total = (own[c, here, :] + y_in[c].astype(F32)).astype(BF16)
        tail = total[:, packs * part :]
        for k in range(packs):
            at = slice(k * part, (k + 1) * part)
            piece = jnp.dot(spread, total[:, at], preferred_element_type=F32)
            piece += jnp.dot(folds[k], tail, preferred_element_type=F32)
            z_out[c, :, at] = piece.astype(BF16)
        for j in range(1, nz):
            to_z(c, j).start()

    def last_step(c):
        total = z_out[c, pl.ds(pl.multiple_of(z * SLAB, SLAB), SLAB), :].astype(F32)
        for j in range(1, nz):
            to_z(c, j).wait_recv()
            total = total + z_in[c, j - 1].astype(F32)
        total = total.astype(BF16)
        tail = jnp.zeros((SLAB, part), F32)
        for k in range(packs):
            tail += jnp.dot(unfolds[k], total[:, k * part : (k + 1) * part], preferred_element_type=F32)
        return jnp.concatenate([total.astype(F32), tail], axis=1)

    pl.loop(0, lat_chunks)(y_step)

    pl.loop(0, 2)(z_step)
    remote(cots.at[y_half_in], cots.at[y_half_in], cfs.at[0], cfr.at[0], y_peer).wait_recv()
    cot_c.start()
    pl.loop(2, lat_chunks)(z_step)
    remote(cots.at[c_half_in], cots.at[c_half_in], cfs.at[1], cfr.at[1], sibling).wait_recv()
    back = lax.dot_general(cots[...], lp[...], NT, preferred_element_type=F32)
    act[...] = jnp.dot(squeeze, (back * slope).astype(BF16), preferred_element_type=F32).astype(BF16)
    g = lat_chunks
    sib_out[g] = lax.dot_general(act[theirs, :], pp[...], NT, preferred_element_type=F32).astype(BF16)
    to_sibling(g).start()
    own[g] = lax.dot_general(act[mine, :], pp[...], NT, preferred_element_type=F32)
    y_step(g)
    z_step(g)

    @pl.loop(0, lat_chunks)
    def _(c):
        latent_ref[:, c_cols(c)] = last_step(c)[:slots].astype(BF16)

    grad_ref[...] = jnp.where(valid, last_step(g), 0.0)[:slots].astype(BF16)

    @pl.when(chip < chips - 1)
    def _():
        @pl.loop(0, groups)
        def _(g):
            ahead(0, g).wait_send()
            ahead(1, g).wait_send()

    @pl.when((core == 0) | (chip >= 1))
    def _():
        @pl.loop(0, groups)
        def _(g):
            across(0, g).wait_send()
            across(1, g).wait_send()

    if exchange:
        p_remote.wait_send()
        l_remote.wait_send()
    for copy in cot_z + pool_z + [cot_y, cot_c, pool_y, pool_c]:
        copy.wait_send()

    @pl.loop(0, chunks)
    def _(c):
        to_sibling(c).wait_send()
        to_y(c).wait_send()
        for j in range(1, nz):
            to_z(c, j).wait_send()


def per_device(
    n,
    exchange,
    byte_queries,
    byte_keys,
    byte_values,
    patch_starts,
    patch_proj,
    latent_proj,
    latent_cotangent,
):
    rows, width = byte_queries.shape[1:]
    slots, wide = latent_cotangent.shape[1:]
    if not exchange:
        patch_proj = lax.all_gather(patch_proj, "dp", axis=0, tiled=True)
        latent_proj = lax.all_gather(latent_proj, "dp", axis=1, tiled=True)
    block = patch_proj.shape[1]
    nz = n // 4
    cw = width
    chunks = wide // cw + 1
    groups = width // 256
    half = n // 2 * slots
    vmem = pl.BlockSpec(memory_space=pltpu.VMEM)
    hbm = pl.BlockSpec(memory_space=pl.ANY)
    dma = pltpu.SemaphoreType.DMA
    latent, grads = pl.pallas_call(
        functools.partial(kernel, n, exchange),
        out_shape=(
            jax.ShapeDtypeStruct((slots, wide), BF16),
            jax.ShapeDtypeStruct((slots, width), BF16),
        ),
        in_specs=[hbm] * 7,
        out_specs=(vmem, vmem),
        scratch_shapes=[
            pltpu.SMEM((1, slots), jnp.int32),
            pltpu.VMEM((rows, width), BF16),
            pltpu.VMEM((rows, width), BF16),
            pltpu.VMEM((rows, width), BF16),
            pltpu.VMEM((slots, wide), BF16),
            pltpu.VMEM((2, rows, width), BF16),
            pltpu.VMEM((2, rows, width), BF16),
            pltpu.VMEM((rows, width), BF16),
            pltpu.VMEM((n * SLAB, width), BF16),
            pltpu.VMEM((n * SLAB, wide), BF16),
            pltpu.VMEM((width, block), BF16),
            pltpu.VMEM((block, wide), BF16),
            pltpu.VMEM((n * slots, block), BF16),
            pltpu.VMEM((chunks, half, cw), F32),
            pltpu.VMEM((chunks, half, cw), BF16),
            pltpu.VMEM((chunks, half, cw), BF16),
            pltpu.VMEM((chunks, half // 2, cw), BF16),
            pltpu.VMEM((chunks, half // 2, cw), BF16),
            pltpu.VMEM((chunks, nz * SLAB, cw * slots // SLAB), BF16),
            pltpu.VMEM((chunks, nz - 1, SLAB, cw * slots // SLAB), BF16),
            dma((5,)),
            dma((2,)),
            dma((2,)),
            dma((2,)),
            dma((2, groups)),
            dma((2, groups)),
            dma((2, groups)),
            dma((2, groups)),
            dma((nz - 1,)),
            dma((nz - 1,)),
            dma((2,)),
            dma((2,)),
            dma((nz - 1,)),
            dma((nz - 1,)),
            dma((2,)),
            dma((2,)),
            dma((chunks,)),
            dma((chunks,)),
            dma((chunks,)),
            dma((chunks,)),
            dma((chunks, nz - 1)),
            dma((chunks, nz - 1)),
        ],
        compiler_params=pltpu.CompilerParams(
            collective_id=0, has_side_effects=True, vmem_limit_bytes=60 * 2**20
        ),
        cost_estimate=pl.CostEstimate(flops=2 * 10**9, bytes_accessed=4 * 10**6, transcendentals=10**6),
    )(
        patch_starts[0],
        byte_queries[0],
        byte_keys[0],
        byte_values[0],
        latent_cotangent[0],
        patch_proj,
        latent_proj,
    )
    return latent[None], grads[None]


def solution(mesh):
    n = mesh.shape["bytes"]
    return jax.shard_map(
        functools.partial(per_device, n, mesh.shape["dp"] == 2),
        mesh=mesh,
        in_specs=(
            P("dp", "bytes", None),
            P("dp", "bytes", None),
            P("dp", "bytes", None),
            P("dp", "bytes", None),
            P("dp", "bytes"),
            P("bytes", "dp"),
            P("dp", "bytes", None),
        ),
        out_specs=(P("dp", "bytes", None), P("dp", "bytes", None)),
        check_vma=False,
    )
```
